128 devices in a mesh: tile: 64 (over y, z_hi, x, core), ch: 2 (over z_lo).
Axes of the slice: x: 4, y: 4, z: 4 (z_hi: 2, z_lo: 2; z = z_hi * 2 + z_lo), core: 2. Of those that a mesh axis runs over, the one named last changes fastest.
Arguments:
- features: bfloat16 [256, 32, 32, 256], P('tile'), may hold values from -6 to 6
- cotangent: bfloat16 [256, 32, 32, 512], P('tile'), may hold values from -6 to 6
- neighbours: int32 [256, 8], P('tile'), may hold values from 0 to 256, as said below
- first_weight: bfloat16 [256, 128], replicated, may hold values from -0.375 to 0.375
- first_bias: float32 [128], replicated, may hold values from -3 to 3
- mid_weight: bfloat16 [3, 3, 128, 128], P(None, None, None, 'ch'), may hold values from -0.1875 to 0.1875
- mid_bias: float32 [128], replicated, may hold values from -3 to 3
- last_weight: bfloat16 [128, 512], P('ch'), may hold values from -0.5 to 0.5
- side_weight: bfloat16 [256, 512], P('ch'), may hold values from -0.375 to 0.375
- last_bias: float32 [512], replicated, may hold values from -3 to 3
Outputs:
- output: bfloat16 [256, 32, 32, 512], P('tile')
- grad_first: float32 [256, 128], P(None, 'ch')
- grad_first_bias: float32 [128], P('ch')
- grad_mid: float32 [3, 3, 128, 128], P(None, None, None, 'ch')
- grad_mid_bias: float32 [128], P('ch')
- grad_last: float32 [128, 512], P('ch')
- grad_side: float32 [256, 512], P('ch')
- grad_last_bias: float32 [512], replicated
The draws below stay inside these ranges and needn't reach their ends.
Inputs may be any that keep to these rules, and one draw needn't show every extreme that they name: `neighbours`: each tissue tile sits at its own position of a window of 16 x 32 tile positions; row t lists the tiles at the positions up-left, up, up-right, left, right, down-left, down, down-right of tile t, or 256 where that position lies outside the window or holds no tissue. The relation is mutual: if u is t's neighbour in a direction, t is u's neighbour in the opposite direction.
All inputs are finite; a program needn't handle non-finite values.
Results may differ from the reference program's by a relative error of at most 0.018.
Values may be sent and summed in bfloat16 or wider, within the bound.
A program may use at most 128 MiB of HBM per device.

```python
import math
import jax
import jax.numpy as jnp
from jax import lax

C_IN = 256
MID = 128
C_OUT = 512
TPD = 4
S = 32
GX = 32
TILES = 256
GRID = 512
GY = 16
GROUPS = 2


DIRECTIONS = ((-1, -1), (-1, 0), (-1, 1), (0, -1), (0, 1), (1, -1), (1, 0), (1, 1))


def draw_neighbours(key, part):
    places = jax.random.permutation(key, GRID)[:TILES].astype(jnp.int32)
    owners = jnp.full((GRID,), TILES, jnp.int32).at[places].set(jnp.arange(TILES, dtype=jnp.int32))
    grid_row = places // GX
    grid_col = places % GX
    columns = []
    for step_row, step_col in DIRECTIONS:
        target_row = grid_row + step_row
        target_col = grid_col + step_col
        inside = (target_row >= 0) & (target_row < GY) & (target_col >= 0) & (target_col < GX)
        target = jnp.clip(target_row, 0, GY - 1) * GX + jnp.clip(target_col, 0, GX - 1)
        columns.append(jnp.where(inside, owners[target], TILES))
    return jnp.stack(columns, axis=1).astype(jnp.int32)


def levels(stream_key, shape, pieces, smallest, top_value):
    loudness = 1.0
    for dim, parts in pieces:
        heights = jax.random.uniform(jax.random.fold_in(jax.random.fold_in(stream_key, 6), dim), (parts,), jnp.float32, smallest / len(pieces), top_value / len(pieces))
        loudness = loudness * jnp.repeat(jnp.exp(heights), shape[dim] // parts).reshape((-1,) + (1,) * (len(shape) - 1 - dim))
    return loudness


def normal_values(key, shape, scale, reach, pieces=(), held_as=jnp.bfloat16):
    loudness = levels(key, shape, pieces, -0.22, 0.18) if pieces else 1.0
    drawn = jax.random.normal(key, shape, jnp.float32) * scale * loudness
    return jnp.minimum(jnp.maximum(drawn, -reach), reach).astype(held_as)


def setup_inputs(seed: int = 0) -> dict:
    splits = jax.random.split(jax.random.key(seed), 11)
    features = normal_values(splits[0], (TILES, S, S, C_IN), 1.0, 6.0, ((0, 64),))
    cotangent = normal_values(splits[1], (TILES, S, S, C_OUT), 1.0, 6.0, ((0, 64),))
    neighbours = draw_neighbours(jax.random.fold_in(splits[10], 71), 0)
    first_weight = normal_values(splits[3], (C_IN, MID), C_IN ** -0.5, 0.375)
    first_bias = normal_values(splits[4], (MID,), 0.5, 3.0, (), jnp.float32)
    mid_weight = normal_values(splits[5], (3, 3, MID, MID), (9 * MID) ** -0.5, 0.1875, ((3, 2),))
    mid_bias = normal_values(splits[6], (MID,), 0.5, 3.0, (), jnp.float32)
    last_weight = normal_values(splits[7], (MID, C_OUT), MID ** -0.5, 0.5, ((0, 2),))
    side_weight = normal_values(splits[8], (C_IN, C_OUT), C_IN ** -0.5, 0.375, ((0, 2),))
    last_bias = normal_values(splits[9], (C_OUT,), 0.5, 3.0, (), jnp.float32)
    return dict(features=features, cotangent=cotangent, neighbours=neighbours, first_weight=first_weight, first_bias=first_bias, mid_weight=mid_weight, mid_bias=mid_bias, last_weight=last_weight, side_weight=side_weight, last_bias=last_bias)


FORWARD_OFFSETS = ((0, 0), (0, 1), (0, 2), (1, 0), (1, 1), (1, 2), (2, 0), (2, 1), (2, 2))
BACKWARD_OFFSETS = ((2, 2), (2, 1), (2, 0), (1, 2), (1, 1), (1, 0), (0, 2), (0, 1), (0, 0))

def silu_slope(values):
    sigma = jax.nn.sigmoid(values)
    return sigma * (1.0 + values * (1.0 - sigma))

def edge_table(tiles_in):
    return jnp.stack([tiles_in[:, 0], tiles_in[:, -1], tiles_in[:, :, 0], tiles_in[:, :, -1]], axis=1)

def assemble(tiles_in, strip_table, neighbours):
    table_size = strip_table.shape[0]

    def choose_strip(direction, strip_id):
        owner_ids = neighbours[:, direction]
        present = owner_ids < table_size
        strips = strip_table[jnp.minimum(owner_ids, table_size - 1), strip_id]
        return jnp.where(present[:, None, None], strips, jnp.zeros_like(strips))
    above_row = choose_strip(1, 1)
    below_row = choose_strip(6, 0)
    left_col = choose_strip(3, 3)
    right_col = choose_strip(4, 2)
    up_left = choose_strip(0, 1)[:, -1:]
    up_right = choose_strip(2, 1)[:, :1]
    down_left = choose_strip(5, 0)[:, -1:]
    down_right = choose_strip(7, 0)[:, :1]
    top_band = jnp.concatenate([up_left, above_row, up_right], axis=1)
    bottom_band = jnp.concatenate([down_left, below_row, down_right], axis=1)
    middle = jnp.concatenate([left_col[:, :, None], tiles_in, right_col[:, :, None]], axis=2)
    return jnp.concatenate([top_band[:, None], middle, bottom_band[:, None]], axis=1)

def patch_cols(padded_in, offset_list):
    extent = padded_in.shape[1] - 2
    return jnp.concatenate([padded_in[:, row_off:row_off + extent, col_off:col_off + extent, :] for row_off, col_off in offset_list], axis=-1)

def reference(features, cotangent, neighbours, first_weight, first_bias, mid_weight, mid_bias, last_weight, side_weight, last_bias):
    tiles_all = features.shape[0]
    extent = features.shape[1]
    block_tiles = TPD
    blocks = tiles_all // block_tiles
    pixels = block_tiles * extent * extent
    scale_loss = 1.0 / math.sqrt(TPD * extent * extent)
    mid_group = MID // GROUPS
    in_group = C_IN // GROUPS

    def first_layer(tile_block):
        flat_in = tile_block.reshape(pixels, C_IN)
        first_pre = jnp.dot(flat_in, first_weight, preferred_element_type=jnp.float32) + first_bias
        return jax.nn.silu(first_pre).astype(jnp.bfloat16).reshape(block_tiles, extent, extent, MID)
    first_act = lax.map(first_layer, features.reshape(blocks, block_tiles, extent, extent, C_IN))
    first_act = first_act.reshape(tiles_all, extent, extent, MID)
    strips_one = edge_table(first_act)
    w_flat = mid_weight.reshape(9 * MID, MID)

    def middle_pass(totals, number):
        first_row = number * block_tiles
        feat_block = lax.dynamic_slice_in_dim(features, first_row, block_tiles, 0)
        cot_block = lax.dynamic_slice_in_dim(cotangent, first_row, block_tiles, 0)
        near_block = lax.dynamic_slice_in_dim(neighbours, first_row, block_tiles, 0)
        act_block = lax.dynamic_slice_in_dim(first_act, first_row, block_tiles, 0)
        padded = assemble(act_block, strips_one, near_block)
        mid_patches = patch_cols(padded, FORWARD_OFFSETS).reshape(pixels, 9 * MID)
        mid_pre = jnp.dot(mid_patches, w_flat, preferred_element_type=jnp.float32) + mid_bias
        mid_act = jax.nn.silu(mid_pre).astype(jnp.bfloat16)
        flat_in = feat_block.reshape(pixels, C_IN)
        out_pre = jnp.zeros((pixels, C_OUT), jnp.float32) + last_bias
        for group in range(GROUPS):
            partial_value = jnp.dot(mid_act[:, group * mid_group:(group + 1) * mid_group], last_weight[group * mid_group:(group + 1) * mid_group], preferred_element_type=jnp.float32)
            partial_value = partial_value + jnp.dot(flat_in[:, group * in_group:(group + 1) * in_group], side_weight[group * in_group:(group + 1) * in_group], preferred_element_type=jnp.float32)
            out_pre = out_pre + lax.optimization_barrier(partial_value.astype(jnp.bfloat16)).astype(jnp.float32)
        output = jax.nn.silu(out_pre).astype(jnp.bfloat16)
        grad_out = (cot_block.reshape(pixels, C_OUT).astype(jnp.float32) * scale_loss * silu_slope(out_pre)).astype(jnp.bfloat16)
        grad_last, grad_side, grad_last_bias, grad_mid, grad_mid_bias = totals
        grad_last = grad_last + jnp.dot(mid_act.T, grad_out, preferred_element_type=jnp.float32)
        grad_side = grad_side + jnp.dot(flat_in.T, grad_out, preferred_element_type=jnp.float32)
        grad_last_bias = grad_last_bias + lax.optimization_barrier(jnp.sum(grad_out.astype(jnp.float32), axis=0))
        mid_back = jnp.dot(grad_out, last_weight.T, preferred_element_type=jnp.float32)
        mid_delta = (mid_back * silu_slope(mid_pre)).astype(jnp.bfloat16)
        grad_mid = grad_mid + jnp.dot(mid_patches.T, mid_delta, preferred_element_type=jnp.float32)
        grad_mid_bias = grad_mid_bias + lax.optimization_barrier(jnp.sum(mid_delta.astype(jnp.float32), axis=0))
        new_totals = (grad_last, grad_side, grad_last_bias, grad_mid, grad_mid_bias)
        return (new_totals, (output.reshape(block_tiles, extent, extent, C_OUT), mid_delta.reshape(block_tiles, extent, extent, MID)))
    start_totals = (jnp.zeros((MID, C_OUT), jnp.float32), jnp.zeros((C_IN, C_OUT), jnp.float32), jnp.zeros((C_OUT,), jnp.float32), jnp.zeros((9 * MID, MID), jnp.float32), jnp.zeros((MID,), jnp.float32))
    totals, stacked = lax.scan(middle_pass, start_totals, jnp.arange(blocks, dtype=jnp.int32))
    grad_last, grad_side, grad_last_bias, grad_mid, grad_mid_bias = totals
    output = stacked[0].reshape(tiles_all, extent, extent, C_OUT)
    mid_delta_all = stacked[1].reshape(tiles_all, extent, extent, MID)
    strips_two = edge_table(mid_delta_all)
    w_back = mid_weight.transpose(0, 1, 3, 2).reshape(9 * MID, MID)

    def lower_pass(totals_low, number):
        first_row = number * block_tiles
        feat_block = lax.dynamic_slice_in_dim(features, first_row, block_tiles, 0)
        near_block = lax.dynamic_slice_in_dim(neighbours, first_row, block_tiles, 0)
        delta_block = lax.dynamic_slice_in_dim(mid_delta_all, first_row, block_tiles, 0)
        delta_padded = assemble(delta_block, strips_two, near_block)
        back_patches = patch_cols(delta_padded, BACKWARD_OFFSETS).reshape(pixels, 9 * MID)
        first_grad = jnp.dot(back_patches, w_back, preferred_element_type=jnp.float32)
        flat_in = feat_block.reshape(pixels, C_IN)
        first_pre = jnp.dot(flat_in, first_weight, preferred_element_type=jnp.float32) + first_bias
        first_delta = (first_grad * silu_slope(first_pre)).astype(jnp.bfloat16)
        grad_first, grad_first_bias = totals_low
        grad_first = grad_first + jnp.dot(flat_in.T, first_delta, preferred_element_type=jnp.float32)
        grad_first_bias = grad_first_bias + lax.optimization_barrier(jnp.sum(first_delta.astype(jnp.float32), axis=0))
        return ((grad_first, grad_first_bias), None)
    low_start = (jnp.zeros((C_IN, MID), jnp.float32), jnp.zeros((MID,), jnp.float32))
    low_totals, unused = lax.scan(lower_pass, low_start, jnp.arange(blocks, dtype=jnp.int32))
    grad_first, grad_first_bias = low_totals
    return (output, grad_first, grad_first_bias, grad_mid.reshape(3, 3, MID, MID), grad_mid_bias, grad_last, grad_side, grad_last_bias)
```

```python
import math

import jax
import jax.numpy as jnp
from jax import lax
from jax.experimental import pallas as pl
from jax.experimental.pallas import tpu as pltpu
from jax.sharding import PartitionSpec as P

BF = jnp.bfloat16
F32 = jnp.float32
MESH = pl.DeviceIdType.MESH

ROW_FIRST = 0
ROW_MID = 128
ROW_LAST = 704
ROW_SIDE = 960
ROW_BIAS = 1472
ROWS = 1536
CORE_ROWS = ROWS // 2
PIECE = CORE_ROWS // 16

CHUNK = 256


def place():
    tile = lax.axis_index("tile")
    ch = lax.axis_index("ch")
    return tile // 16, (tile // 8) % 2, (tile // 2) % 4, tile % 2, ch


def device(y, zh, x, core, ch):
    return (((y * 2 + zh) * 4 + x) * 2 + core, ch)


def exchange_kernel(
    feat,
    near,
    wb_own,
    wl_own,
    ws_own,
    halo,
    wb_other,
    wl_other,
    ws_other,
    wide,
    edges,
    table,
    table_s,
    every,
    pack,
    got,
    piece,
    send_sem,
    recv_sem,
    local_sem,
):
    y, zh, x, core, ch = place()
    along = jnp.where(core == 0, x, y)
    across = jnp.where(core == 0, y, x)

    def gather_peer(step):
        to = lax.rem(along + step, 4)
        return device(jnp.where(core == 0, y, to), zh, jnp.where(core == 0, to, x), core, ch)

    def select_peer(step):
        to = lax.rem(across + step, 4)
        return device(jnp.where(core == 0, to, y), zh, jnp.where(core == 0, x, to), core, ch)

    sibling = device(y, zh, x, 1 - core, ch)
    z_peers = [device(y, 1 - zh, x, role, 1 - ch) for role in (0, 1)]
    z_same = device(y, 1 - zh, x, core, 1 - ch)
    z_cross = device(y, 1 - zh, x, 1 - core, 1 - ch)
    ch_same = device(y, zh, x, core, 1 - ch)
    ch_cross = device(y, zh, x, 1 - core, 1 - ch)

    barrier = pltpu.get_barrier_semaphore()
    greeted = [sibling, z_same, z_cross, ch_same, ch_cross]
    greeted += [gather_peer(1), gather_peer(3)]
    greeted += [select_peer(1), select_peer(2), select_peer(3)]
    for peer in greeted:
        pl.semaphore_signal(barrier, inc=1, device_id=peer, device_id_type=MESH)

    table[across, core] = jnp.zeros((8, 128), jnp.int32)
    table[across, core, 0:4, 0:8] = near[...]

    for tile in range(4):
        first_row = feat[tile, 0]
        last_row = feat[tile, 31]
        for half in range(2):
            lanes = slice(half * 128, half * 128 + 128)
            wide[0:512, :] = feat[tile, :, 0:16, lanes].astype(F32).reshape(512, 128)
            wide[512:1024, :] = feat[tile, :, 16:32, lanes].astype(F32).reshape(512, 128)
            edges[0, half, tile, 0] = first_row[:, lanes]
            edges[0, half, tile, 1] = last_row[:, lanes]
            edges[1, half, tile, 0] = wide[pl.ds(0, 32, stride=16), :].astype(BF)
            edges[1, half, tile, 1] = wide[pl.ds(527, 32, stride=16), :].astype(BF)
    every[zh, along, core] = edges[core, ch]

    pl.semaphore_wait(barrier, len(greeted))

    def copy(number, source, target, peer, arrives):
        return pltpu.make_async_remote_copy(
            src_ref=source,
            dst_ref=target,
            send_sem=send_sem.at[number],
            recv_sem=recv_sem.at[arrives],
            device_id=peer,
            device_id_type=MESH,
        )

    sent = []

    def start(number, source, target, peer, arrives):
        made = copy(number, source, target, peer, arrives)
        made.start()
        sent.append(made)
        return made

    tab = start(0, table.at[across, core], table.at[across_of(1 - core, x, y), core], sibling, 0)
    sib_along = jnp.where(core == 0, y, x)
    start(1, edges.at[1 - core, ch], every.at[zh, sib_along, core], sibling, 1)
    for role in range(2):
        place_along = x if role == 0 else y
        start(
            2 + role,
            edges.at[role, 1 - ch],
            every.at[zh, place_along, core],
            z_peers[role],
            2 + core,
        )
    start(4, wb_own, wb_other, ch_same, 4)
    start(5, wl_own, wl_other, ch_same, 5)
    start(6, ws_own, ws_other, ch_same, 6)

    def arrived(number, target):
        copy(0, target, target, sibling, number).wait_recv()

    arrived(1, every.at[zh, along, 1 - core])
    start(7, every.at[zh, along], every.at[zh, along], gather_peer(1), 7)
    start(8, every.at[zh, along], every.at[zh, along], gather_peer(3), 8)
    arrived(0, table.at[across, 1 - core])
    for step in range(1, 4):
        start(8 + step, table.at[across], table.at[across], select_peer(step), 8 + step)
    arrived(2, every.at[1 - zh, along, 0])
    arrived(3, every.at[1 - zh, along, 1])
    start(12, every.at[1 - zh, along], every.at[1 - zh, along], gather_peer(1), 12)
    start(13, every.at[1 - zh, along], every.at[1 - zh, along], gather_peer(3), 13)
    before = lax.rem(along + 3, 4)
    after = lax.rem(along + 1, 4)
    opposite = lax.rem(along + 2, 4)
    for plane, first, second in ((zh, 7, 14), (1 - zh, 12, 16)):
        arrived(first, every.at[plane, before])
        start(
            second, every.at[plane, before, 0], every.at[plane, before, 0], gather_peer(1), second
        )
        arrived(first + 1, every.at[plane, after])
        start(
            second + 1,
            every.at[plane, after, 1],
            every.at[plane, after, 1],
            gather_peer(3),
            second + 1,
        )
    for step in range(1, 4):
        arrived(8 + step, table.at[lax.rem(across + 4 - step, 4)])
    local = pltpu.make_async_copy(table, table_s, local_sem)
    local.start()
    local.wait()
    for second, plane in ((14, zh), (16, 1 - zh)):
        arrived(second, every.at[plane, opposite, 0])
        arrived(second + 1, every.at[plane, opposite, 1])

    first_dir = 1 + 2 * core
    second_dir = 6 - 2 * core
    rows16 = lax.broadcasted_iota(jnp.int32, (16, 128), 0)

    def strip(tile_id, which, rows=slice(0, 32)):
        n = jnp.minimum(tile_id, 255)
        held_along = jnp.where(core == 0, (n // 8) % 4, n // 64)
        return every[(n // 32) % 2, held_along, (n // 4) % 2, n % 4, which, rows, :]

    def source(tile_id):
        n = jnp.minimum(tile_id, 255)
        return jnp.where(core == 0, n // 64, (n // 8) % 4)

    for step in (1, 3, 2, 0):
        wanted = lax.rem(across + step, 4)

        def pack_tile(number, carry, wanted=wanted, step=step):
            owner, tile = number // 4, number % 4
            ids = lambda d: table_s[wanted, owner, tile, d]
            one = strip(ids(first_dir), 1)
            two = strip(ids(second_dir), 0)
            up_left = strip(ids(0), 1, slice(16, 32)).astype(F32)[15:16]
            up_right = strip(ids(2), 1, slice(0, 16)).astype(F32)[0:1]
            down_left = strip(ids(5), 0, slice(16, 32)).astype(F32)[15:16]
            down_right = strip(ids(7), 0, slice(0, 16)).astype(F32)[0:1]
            corners = jnp.where(
                rows16 == 0,
                up_left,
                jnp.where(
                    rows16 == 1,
                    up_right,
                    jnp.where(rows16 == 2, down_left, jnp.where(rows16 == 3, down_right, 0.0)),
                ),
            )
            pack[step, owner, tile, 0:32, :] = one
            pack[step, owner, tile, 32:64, :] = two
            pack[step, owner, tile, 64:80, :] = corners.astype(BF)
            return carry

        lax.fori_loop(0, 8, pack_tile, 0)
        if step:
            start(17 + step, pack.at[step], got.at[step], select_peer(step), 17 + step)
    for step in range(1, 4):
        arrived(17 + step, got.at[step])

    def take(tile_id):
        return lax.rem(across + 4 - source(tile_id), 4)

    def finish_tile(number, carry):
        owner, tile = number // 4, number % 4
        ids = lambda d: table_s[across, owner, tile, d]

        def chosen(d, rows):
            return got[take(ids(d)), owner, tile, rows, :]

        one = chosen(first_dir, slice(0, 32))
        two = chosen(second_dir, slice(32, 64))
        end = slice(64, 80)
        corners = jnp.where(
            rows16 == 0,
            chosen(0, end).astype(F32),
            jnp.where(
                rows16 == 1,
                chosen(2, end).astype(F32),
                jnp.where(rows16 == 2, chosen(5, end).astype(F32), chosen(7, end).astype(F32)),
            ),
        )
        piece[owner, tile, 0:32, :] = one
        piece[owner, tile, 32:64, :] = two
        piece[owner, tile, 64:80, :] = corners.astype(BF)
        return carry

    got[0] = pack[0]
    lax.fori_loop(0, 8, finish_tile, 0)
    halo[core, ch] = piece[core]
    start(21, piece.at[1 - core], halo.at[core, ch], sibling, 21)
    start(22, piece.at[core], halo.at[core, ch], ch_same, 22)
    start(23, piece.at[1 - core], halo.at[core, ch], ch_cross, 23)
    arrived(21, halo.at[1 - core, ch])
    arrived(22, halo.at[core, 1 - ch])
    arrived(23, halo.at[1 - core, 1 - ch])
    arrived(4, wb_other)
    arrived(5, wl_other)
    arrived(6, ws_other)
    for made in sent:
        made.wait_send()


def across_of(core, x, y):
    return jnp.where(core == 0, y, x)


def exchange(features, neighbours, wb_own, wl_own, ws_own):
    vmem = pl.BlockSpec(memory_space=pltpu.VMEM)
    return pl.pallas_call(
        exchange_kernel,
        out_shape=(
            jax.ShapeDtypeStruct((2, 2, 4, 80, 128), BF),
            jax.ShapeDtypeStruct(wb_own.shape, BF),
            jax.ShapeDtypeStruct(wl_own.shape, BF),
            jax.ShapeDtypeStruct(ws_own.shape, BF),
        ),
        in_specs=[vmem] * 5,
        out_specs=(vmem,) * 4,
        scratch_shapes=[
            pltpu.VMEM((1024, 128), F32),
            pltpu.VMEM((2, 2, 4, 2, 32, 128), BF),
            pltpu.VMEM((4, 2, 8, 128), jnp.int32),
            pltpu.SMEM((4, 2, 8, 128), jnp.int32),
            pltpu.VMEM((2, 4, 2, 4, 2, 32, 128), BF),
            pltpu.VMEM((4, 2, 4, 80, 128), BF),
            pltpu.VMEM((4, 2, 4, 80, 128), BF),
            pltpu.VMEM((2, 4, 80, 128), BF),
            pltpu.SemaphoreType.DMA((24,)),
            pltpu.SemaphoreType.DMA((24,)),
            pltpu.SemaphoreType.DMA,
        ],
        compiler_params=pltpu.CompilerParams(
            collective_id=0, has_side_effects=True, vmem_limit_bytes=48 * 2**20
        ),
    )(features, neighbours, wb_own, wl_own, ws_own)


def sigmoid(v):
    return 0.5 + 0.5 * jnp.tanh(0.5 * v)


def dot(a, b):
    return jnp.dot(a, b, preferred_element_type=F32)


def dot_nt(a, b):
    return lax.dot_general(a, b, (((1,), (1,)), ((), ())), preferred_element_type=F32)


def dot_tn(a, b):
    return lax.dot_general(a, b, (((0,), (0,)), ((), ())), preferred_element_type=F32)


def compute_kernel(
    scale,
    ch_s,
    near_s,
    feat,
    cot,
    halo,
    w1,
    b1,
    wb_own,
    wb_other,
    mid_bias,
    wl_own,
    wl_other,
    ws_own,
    ws_other,
    last_bias,
    out,
    grads,
    wf,
    wbt,
    wl,
    ws,
    first_pre,
    side_pre,
    padded,
    patches,
    mid_delta,
    spread,
    rim,
    g_first,
    g_mid,
    g_last,
    g_side,
    g_first_bias,
    g_mid_bias,
    g_last_bias,
):
    step = pl.program_id(0)
    ch = ch_s[0]
    tile = lax.rem(step + 2 * ch, 4)
    own64 = pl.multiple_of(ch * 64, 64)
    other64 = pl.multiple_of((1 - ch) * 64, 64)
    own128 = pl.multiple_of(ch * 128, 128)
    other128 = pl.multiple_of((1 - ch) * 128, 128)

    @pl.when(step == 0)
    def _():
        for i in range(3):
            lanes = slice(i * 384, i * 384 + 384)
            rows = jnp.concatenate([wb_own[:, lanes], wb_other[:, lanes]], axis=0)
            wbt[i * 128 : i * 128 + 128, :] = rows
            wf[i] = rows.astype(F32).T.astype(BF)
        wl[0:64, :] = wl_own[...]
        wl[64:128, :] = wl_other[...]
        ws[pl.ds(own128, 128), :] = ws_own[...]
        ws[pl.ds(other128, 128), :] = ws_other[...]
        for ref in (g_first, g_mid, g_last, g_side, g_first_bias, g_mid_bias, g_last_bias):
            ref[...] = jnp.zeros_like(ref)

    def here(direction):
        return jnp.where(near_s[tile, direction] < 256, 1.0, 0.0).astype(F32)

    x_own = feat[...]
    pre = dot(x_own, w1[...]) + b1[...]
    first_pre[...] = pre
    act = pre * sigmoid(pre)
    padded[1:33, 8:40, :] = act.reshape(32, 32, 128)
    x_rim = jnp.concatenate(
        [
            jnp.concatenate([halo[0, 0, 0], halo[0, 1, 0]], axis=1),
            jnp.concatenate([halo[1, 0, 0], halo[1, 1, 0]], axis=1),
        ],
        axis=0,
    )
    pre = dot(x_rim, w1[...]) + b1[...]
    side_pre[...] = pre
    act = pre * sigmoid(pre)
    padded[0, 8:40, :] = act[0:32] * here(1)
    padded[33, 8:40, :] = act[32:64] * here(6)
    rim[...] = act
    padded[1:33, 7:8, :] = (act[80:112] * here(3)).reshape(32, 1, 128)
    padded[1:33, 40:41, :] = (act[112:144] * here(4)).reshape(32, 1, 128)
    padded[0, 7:8, :] = rim[64:65, :] * here(0)
    padded[0, 40:41, :] = rim[65:66, :] * here(2)
    padded[33, 7:8, :] = rim[66:67, :] * here(5)
    padded[33, 40:41, :] = rim[67:68, :] * here(7)
    for j in range(3):
        patches[:, :, j * 128 : j * 128 + 128] = padded[:, 7 + j : 39 + j, :].astype(BF)

    def forward(number):
        row = pl.multiple_of(number * CHUNK, CHUNK)
        high = CHUNK // 32
        line = number * high
        views = [patches[pl.ds(line + i, high)].reshape(CHUNK, 384) for i in range(3)]
        mid_pre = mid_bias[...] + dot(views[0], wf[0]) + dot(views[1], wf[1]) + dot(views[2], wf[2])
        mid_sig = sigmoid(mid_pre)
        mid_val = mid_pre * mid_sig
        mid_act = mid_val.astype(BF)
        x_part = feat[pl.ds(row, CHUNK), :]
        out_pre = dot(mid_act, wl[...]) + dot(x_part, ws[...]) + last_bias[...]
        sig = sigmoid(out_pre)
        val = out_pre * sig
        out[pl.ds(row, CHUNK), :] = val.astype(BF)
        return row, views, mid_sig, mid_val, mid_act, x_part, sig, val

    @pl.when(step >= 2)
    def _():
        def body(number, carry):
            forward(number)
            return carry

        lax.fori_loop(0, 1024 // CHUNK, body, 0)

    @pl.when(step < 2)
    def _():
        def body(number, carry):
            row, views, mid_sig, mid_val, mid_act, x_part, sig, val = forward(number)
            slope = sig + val * (1.0 - sig)
            grad_out = (cot[pl.ds(row, CHUNK), :].astype(F32) * scale * slope).astype(BF)
            g_last[...] += dot_tn(mid_act, grad_out)
            g_side[...] += dot_tn(x_part, grad_out)
            g_last_bias[...] += grad_out.astype(F32).reshape(CHUNK // 8, 8, 512).sum(axis=0)
            mid_back = dot_nt(grad_out, wl[...])
            delta = (mid_back * (mid_sig + mid_val * (1.0 - mid_sig))).astype(BF)
            g_mid_bias[...] += delta.astype(F32).reshape(CHUNK // 8, 8, 128).sum(axis=0)
            for i in range(3):
                g_mid[i] += dot_tn(delta, views[i])
            high = CHUNK // 32
            line = number * high
            for i in range(3):
                mid_delta[pl.ds(line + i, high), :, i * 128 : i * 128 + 128] = delta.reshape(
                    high, 32, 128
                )
            return carry

        blank = jnp.zeros((32, 128), BF)
        mid_delta[32, :, 0:128] = blank
        mid_delta[33, :, 0:128] = blank
        mid_delta[0, :, 128:256] = blank
        mid_delta[33, :, 128:256] = blank
        mid_delta[0, :, 256:384] = blank
        mid_delta[1, :, 256:384] = blank
        lax.fori_loop(0, 1024 // CHUNK, body, 0)

        back = dot(mid_delta[...].reshape(1088, 384), wbt[...]).reshape(34, 32, 384)
        spread[:, 0:8, :] = jnp.zeros((34, 8, 128), F32)
        spread[:, 40:48, :] = jnp.zeros((34, 8, 128), F32)
        spread[:, 8:40, :] = back[:, :, 128:256]
        spread[:, 7:39, :] += back[:, :, 0:128]
        spread[:, 9:41, :] += back[:, :, 256:384]

        pre = first_pre[...]
        sig = sigmoid(pre)
        slope = sig + pre * sig * (1.0 - sig)
        delta = (spread[1:33, 8:40, :].reshape(1024, 128) * slope).astype(BF)
        rim[...] = jnp.zeros_like(rim)
        rim[0:32, :] = spread[0, 8:40, :] * here(1)
        rim[32:64, :] = spread[33, 8:40, :] * here(6)
        rim[64:65, :] = spread[0, 7:8, :] * here(0)
        rim[65:66, :] = spread[0, 40:41, :] * here(2)
        rim[66:67, :] = spread[33, 7:8, :] * here(5)
        rim[67:68, :] = spread[33, 40:41, :] * here(7)
        rim[80:112, :] = spread[1:33, 7:8, :].reshape(32, 128) * here(3)
        rim[112:144, :] = spread[1:33, 40:41, :].reshape(32, 128) * here(4)
        pre = side_pre[...]
        sig = sigmoid(pre)
        slope = sig + pre * sig * (1.0 - sig)
        delta_rim = (rim[...] * slope).astype(BF)
        g_first[...] += dot_tn(delta, x_own) + dot_tn(delta_rim, x_rim)
        g_first_bias[...] += delta.astype(F32).reshape(128, 8, 128).sum(axis=0)
        g_first_bias[...] += delta_rim.astype(F32).reshape(20, 8, 128).sum(axis=0)

    @pl.when(step == 1)
    def _():
        bias_first = jnp.sum(g_first_bias[...], axis=0, keepdims=True)
        bias_mid = jnp.sum(g_mid_bias[...], axis=0, keepdims=True)
        bias_last = jnp.sum(g_last_bias[...], axis=0, keepdims=True)
        rows16 = lax.broadcasted_iota(jnp.int32, (16, 128), 0)
        for half in range(2):
            start64 = own64 if half == 0 else other64
            start128 = own128 if half == 0 else other128
            order = slice(half * 64, half * 64 + 64)
            for k in range(2):
                at = ROW_FIRST + k * 64
                grads[half, at : at + 64, :] = g_first[
                    pl.ds(start64, 64), k * 128 : k * 128 + 128
                ].astype(BF)
            for i in range(3):
                for j in range(3):
                    at = ROW_MID + (i * 3 + j) * 64
                    grads[half, at : at + 64, :] = g_mid[i, order, j * 128 : j * 128 + 128].astype(
                        BF
                    )
            for k in range(4):
                lanes = slice(k * 128, k * 128 + 128)
                at = ROW_LAST + k * 64
                grads[half, at : at + 64, :] = g_last[order, lanes].astype(BF)
                at = ROW_SIDE + k * 128
                grads[half, at : at + 128, :] = g_side[pl.ds(start128, 128), lanes].astype(BF)
            mid_row = bias_mid
            if half == 1:
                mid_row = jnp.concatenate([bias_mid[:, 64:128], bias_mid[:, 0:64]], axis=1)
            rows = jnp.where(rows16 == 0, bias_first, jnp.where(rows16 == 1, mid_row, 0.0))
            for k in range(4):
                rows = jnp.where(rows16 == 2 + k, bias_last[:, k * 128 : k * 128 + 128], rows)
            grads[half, ROW_BIAS : ROW_BIAS + 16, :] = rows.astype(BF)
            grads[half, ROW_BIAS + 16 : ROWS, :] = jnp.zeros((ROWS - ROW_BIAS - 16, 128), BF)


def compute(
    scale,
    ch,
    neighbours,
    features,
    cotangent,
    halo,
    w1,
    b1,
    wb_own,
    wb_other,
    mid_bias,
    wl_own,
    wl_other,
    ws_own,
    ws_other,
    last_bias,
):
    def whole(shape):
        zeros = (0,) * len(shape)
        return pl.BlockSpec(shape, lambda s, c, n: zeros)

    def tile_at(s, c):
        return lax.rem(s + 2 * c[0], 4)

    grid_spec = pltpu.PrefetchScalarGridSpec(
        num_scalar_prefetch=2,
        grid=(4,),
        in_specs=[
            pl.BlockSpec((1024, 256), lambda s, c, n: (tile_at(s, c), 0)),
            pl.BlockSpec((1024, 512), lambda s, c, n: (2 * c[0] + jnp.minimum(s, 1), 0)),
            pl.BlockSpec((2, 2, 1, 80, 128), lambda s, c, n: (0, 0, tile_at(s, c), 0, 0)),
            whole((256, 128)),
            whole((1, 128)),
            whole((64, 1152)),
            whole((64, 1152)),
            whole((1, 128)),
            whole((64, 512)),
            whole((64, 512)),
            whole((128, 512)),
            whole((128, 512)),
            whole((1, 512)),
        ],
        out_specs=(
            pl.BlockSpec((1024, 512), lambda s, c, n: (tile_at(s, c), 0)),
            whole((2, ROWS, 128)),
        ),
        scratch_shapes=[
            pltpu.VMEM((3, 384, 128), BF),
            pltpu.VMEM((384, 384), BF),
            pltpu.VMEM((128, 512), BF),
            pltpu.VMEM((256, 512), BF),
            pltpu.VMEM((1024, 128), F32),
            pltpu.VMEM((160, 128), F32),
            pltpu.VMEM((34, 48, 128), F32),
            pltpu.VMEM((34, 32, 384), BF),
            pltpu.VMEM((34, 32, 384), BF),
            pltpu.VMEM((34, 48, 128), F32),
            pltpu.VMEM((160, 128), F32),
            pltpu.VMEM((128, 256), F32),
            pltpu.VMEM((3, 128, 384), F32),
            pltpu.VMEM((128, 512), F32),
            pltpu.VMEM((256, 512), F32),
            pltpu.VMEM((8, 128), F32),
            pltpu.VMEM((8, 128), F32),
            pltpu.VMEM((8, 512), F32),
        ],
    )

    def kernel(*refs):
        compute_kernel(scale, *refs)

    return pl.pallas_call(
        kernel,
        grid_spec=grid_spec,
        out_shape=(
            jax.ShapeDtypeStruct((4096, 512), BF),
            jax.ShapeDtypeStruct((2, ROWS, 128), BF),
        ),
        compiler_params=pltpu.CompilerParams(vmem_limit_bytes=56 * 2**20),
    )(
        ch,
        neighbours,
        features,
        cotangent,
        halo,
        w1,
        b1,
        wb_own,
        wb_other,
        mid_bias,
        wl_own,
        wl_other,
        ws_own,
        ws_other,
        last_bias,
    )


def reduce_kernel(grads, total, from_core, by_piece, from_plane, mine, from_z, done, send_sem, recv_sem):
    y, zh, x, core, ch = place()
    own = y * 4 + x
    sibling = device(y, zh, x, 1 - core, ch)

    def plane_peer(step):
        to = lax.rem(own + step, 16)
        return device(to // 4, zh, to % 4, core, ch)

    z_same = device(y, 1 - zh, x, core, ch)
    ch_same = device(y, zh, x, core, 1 - ch)
    z_cross = device(y, 1 - zh, x, core, 1 - ch)
    last = [z_same, ch_same, z_cross]

    barrier = pltpu.get_barrier_semaphore()
    greeted = [sibling, *last] + [plane_peer(step) for step in range(1, 16)]
    for peer in greeted:
        pl.semaphore_signal(barrier, inc=1, device_id=peer, device_id_type=MESH)
    pl.semaphore_wait(barrier, len(greeted))

    def copy(number, source, target, peer):
        return pltpu.make_async_remote_copy(
            src_ref=source,
            dst_ref=target,
            send_sem=send_sem.at[number],
            recv_sem=recv_sem.at[number],
            device_id=peer,
            device_id_type=MESH,
        )

    own_rows = pl.multiple_of(core * CORE_ROWS, CORE_ROWS)
    other_rows = pl.multiple_of((1 - core) * CORE_ROWS, CORE_ROWS)
    swap = copy(0, grads.at[:, pl.ds(other_rows, CORE_ROWS)], from_core, sibling)
    swap.start()
    swap.wait()
    for half in range(2):
        added = grads[half, pl.ds(own_rows, CORE_ROWS), :].astype(F32) + from_core[half].astype(F32)
        by_piece[:, half] = added.astype(BF).reshape(16, PIECE, 128)
    copies = []
    for step in range(1, 16):
        to = lax.rem(own + step, 16)
        made = copy(step, by_piece.at[to], from_plane.at[step], plane_peer(step))
        made.start()
        copies.append(made)
    added = by_piece[own].astype(F32)
    for step, made in enumerate(copies, 1):
        made.wait_recv()
        added = added + from_plane[step].astype(F32)
    mine[...] = added.astype(BF)
    halves = (0, 1, 1)
    hops = []
    for k in range(3):
        made = copy(16 + k, mine.at[halves[k]], from_z.at[k], last[k])
        made.start()
        hops.append(made)
    added = added[0]
    for k, made in enumerate(hops):
        made.wait_recv()
        added = added + from_z[k].astype(F32)
    at = own_rows + own * PIECE
    at = pl.multiple_of(at, 16)
    done[pl.ds(at, PIECE), :] = added.astype(BF)
    backs = []
    for step in range(1, 16):
        made = copy(18 + step, done.at[pl.ds(at, PIECE)], done.at[pl.ds(at, PIECE)], plane_peer(step))
        made.start()
        backs.append(made)
    for made in backs:
        made.wait_recv()
    final = copy(34, done.at[pl.ds(own_rows, CORE_ROWS)], done.at[pl.ds(own_rows, CORE_ROWS)], sibling)
    final.start()
    final.wait_recv()
    total[...] = done[...]
    for made in [*copies, *hops, *backs, final]:
        made.wait_send()


def reduce_gradients(grads):
    vmem = pl.BlockSpec(memory_space=pltpu.VMEM)
    return pl.pallas_call(
        reduce_kernel,
        out_shape=jax.ShapeDtypeStruct((ROWS, 128), BF),
        in_specs=[vmem],
        out_specs=vmem,
        scratch_shapes=[
            pltpu.VMEM((2, CORE_ROWS, 128), BF),
            pltpu.VMEM((16, 2, PIECE, 128), BF),
            pltpu.VMEM((16, 2, PIECE, 128), BF),
            pltpu.VMEM((2, PIECE, 128), BF),
            pltpu.VMEM((3, PIECE, 128), BF),
            pltpu.VMEM((ROWS, 128), BF),
            pltpu.SemaphoreType.DMA((35,)),
            pltpu.SemaphoreType.DMA((35,)),
        ],
        compiler_params=pltpu.CompilerParams(
            collective_id=1, has_side_effects=True, vmem_limit_bytes=32 * 2**20
        ),
    )(grads)


def unpack_kernel(ch_s, total, g_first, g_first_bias, g_mid, g_mid_bias, g_last, g_side, g_last_bias):
    def rows(at, count):
        return total[at : at + count, :].astype(F32)

    for k in range(2):
        g_first[k * 128 : k * 128 + 128, :] = rows(ROW_FIRST + k * 64, 64).T
    for k in range(9):
        g_mid[k // 3, k % 3] = rows(ROW_MID + k * 64, 64).T
    bias = rows(ROW_BIAS, 16)
    for k in range(4):
        lanes = slice(k * 128, k * 128 + 128)
        g_last[:, lanes] = rows(ROW_LAST + k * 64, 64)
        g_side[:, lanes] = rows(ROW_SIDE + k * 128, 128)
        g_last_bias[:, lanes] = bias[2 + k : 3 + k, :]
    g_first_bias[...] = jnp.where(ch_s[0] == 0, bias[0:1, 0:64], bias[0:1, 64:128])
    g_mid_bias[...] = bias[1:2, 0:64]


def unpack(ch, total):
    vmem = pl.BlockSpec(memory_space=pltpu.VMEM)
    return pl.pallas_call(
        unpack_kernel,
        in_specs=[pl.BlockSpec(memory_space=pltpu.SMEM), vmem],
        out_specs=(vmem,) * 7,
        out_shape=tuple(
            jax.ShapeDtypeStruct(shape, F32)
            for shape in (
                (256, 64),
                (1, 64),
                (3, 3, 128, 64),
                (1, 64),
                (64, 512),
                (128, 512),
                (1, 512),
            )
        ),
        compiler_params=pltpu.CompilerParams(vmem_limit_bytes=32 * 2**20),
    )(ch, total)


def per_device(
    features,
    cotangent,
    neighbours,
    first_weight,
    first_bias,
    mid_weight,
    mid_bias,
    last_weight,
    side_weight,
    last_bias,
):
    scale = 1.0 / math.sqrt(4096)
    which = lax.axis_index("ch")
    ch = which.astype(jnp.int32).reshape(1)
    wb_own = mid_weight.transpose(3, 0, 1, 2).reshape(64, 1152)
    swapped = jnp.concatenate([mid_bias[64:], mid_bias[:64]])
    own_first = jnp.where(which == 0, mid_bias, swapped).reshape(1, 128)
    halo, wb_other, wl_other, ws_other = exchange(
        features, neighbours, wb_own, last_weight, side_weight
    )
    output, grads = compute(
        scale,
        ch,
        neighbours,
        features.reshape(4096, 256),
        cotangent.reshape(4096, 512),
        halo,
        first_weight,
        first_bias.reshape(1, 128),
        wb_own,
        wb_other,
        own_first,
        last_weight,
        wl_other,
        side_weight,
        ws_other,
        last_bias.reshape(1, 512),
    )
    total = reduce_gradients(grads)
    g_first, g_first_bias, g_mid, g_mid_bias, g_last, g_side, g_last_bias = unpack(ch, total)
    return (
        output.reshape(4, 32, 32, 512),
        g_first,
        g_first_bias.reshape(64),
        g_mid,
        g_mid_bias.reshape(64),
        g_last,
        g_side,
        g_last_bias.reshape(512),
    )


def solution(mesh):
    return jax.shard_map(
        per_device,
        mesh=mesh,
        in_specs=(
            P("tile", None, None, None),
            P("tile", None, None, None),
            P("tile", None),
            P(),
            P(),
            P(None, None, None, "ch"),
            P(),
            P("ch", None),
            P("ch", None),
            P(),
        ),
        out_specs=(
            P("tile", None, None, None),
            P(None, "ch"),
            P("ch"),
            P(None, None, None, "ch"),
            P("ch"),
            P("ch", None),
            P("ch", None),
            P(),
        ),
        check_vma=False,
    )
```

```python
import math

import jax
import jax.numpy as jnp
from jax import lax
from jax.experimental import pallas as pl
from jax.experimental.pallas import tpu as pltpu
from jax.sharding import PartitionSpec as P

BF = jnp.bfloat16
F32 = jnp.float32
MESH = pl.DeviceIdType.MESH

ROW_FIRST = 0
ROW_MID = 128
ROW_LAST = 704
ROW_SIDE = 960
ROW_BIAS = 1472
ROWS = 1536
CORE_ROWS = ROWS // 2
PIECE = CORE_ROWS // 16

CHUNK = 512
PARTS = 8


def place():
    tile = lax.axis_index("tile")
    ch = lax.axis_index("ch")
    return tile // 16, (tile // 8) % 2, (tile // 2) % 4, tile % 2, ch


def device(y, zh, x, core, ch):
    return (((y * 2 + zh) * 4 + x) * 2 + core, ch)


def sigmoid(v):
    return 0.5 + 0.5 * jnp.tanh(0.5 * v)


def dot(a, b):
    return jnp.dot(a, b, preferred_element_type=F32)


def dot_nt(a, b):
    return lax.dot_general(a, b, (((1,), (1,)), ((), ())), preferred_element_type=F32)


def dot_tn(a, b):
    return lax.dot_general(a, b, (((0,), (0,)), ((), ())), preferred_element_type=F32)


def block_kernel(
    scale,
    features,
    cotangent,
    neighbours,
    w1_h,
    b1_h,
    wm_h,
    mid_bias_h,
    wl_h,
    ws_h,
    last_bias_h,
    output,
    total,
    feat,
    cot,
    near,
    near_s,
    w1,
    b1,
    wm,
    mid_bias_n,
    wl_part,
    ws_part,
    last_bias,
    wide,
    edges,
    table,
    table_out,
    table_s,
    every,
    pack,
    got,
    piece,
    halo,
    mid_bias,
    wf,
    wbt,
    wl,
    ws,
    first_pre,
    rim_pre,
    padded,
    patches,
    mid_delta,
    spread,
    rim,
    out,
    g_first,
    g_mid,
    g_last,
    g_side,
    g_first_bias,
    g_mid_bias,
    g_last_bias,
    grads,
    from_core,
    by_piece,
    from_plane,
    mine,
    from_z,
    done,
    local_sem,
    out_sem,
    send_sem,
    recv_sem,
    sum_send_sem,
    sum_recv_sem,
):
    y, zh, x, core, ch = place()
    row_role = core == 0
    along = jnp.where(row_role, x, y)
    across = jnp.where(row_role, y, x)
    own_place = y * 4 + x

    def gather_peer(step):
        to = lax.rem(along + step, 4)
        return device(jnp.where(row_role, y, to), zh, jnp.where(row_role, to, x), core, ch)

    def select_peer(step):
        to = lax.rem(across + step, 4)
        return device(jnp.where(row_role, to, y), zh, jnp.where(row_role, x, to), core, ch)

    def plane_peer(step):
        to = lax.rem(own_place + step, 16)
        return device(to // 4, zh, to % 4, core, ch)

    sibling = device(y, zh, x, 1 - core, ch)
    z_peers = [device(y, 1 - zh, x, role, 1 - ch) for role in (0, 1)]
    ch_same = device(y, zh, x, core, 1 - ch)
    ch_cross = device(y, zh, x, 1 - core, 1 - ch)
    z_even = device(y, 1 - zh, x, core, ch)
    z_odd = device(y, 1 - zh, x, core, 1 - ch)

    barrier = pltpu.get_barrier_semaphore()
    greeted = [sibling, *z_peers, ch_same, ch_cross, z_even]
    greeted += [plane_peer(step) for step in range(1, 16)]
    for peer in greeted:
        pl.semaphore_signal(barrier, inc=1, device_id=peer, device_id_type=MESH)

    loads = [
        (neighbours, near),
        (neighbours, near_s),
        *[(features.at[tile], feat.at[tile]) for tile in range(4)],
        (w1_h, w1),
        (b1_h, b1),
        (wm_h, wm.at[0]),
        (wl_h, wl_part.at[0]),
        (ws_h, ws_part.at[0]),
        (mid_bias_h, mid_bias_n),
        (last_bias_h, last_bias),
    ]
    loads += [
        (cotangent.at[pl.ds(pl.multiple_of((2 * ch + k) * 1024, 1024), 1024)], cot.at[k])
        for k in range(2)
    ]
    loading = []
    for number, (source, target) in enumerate(loads):
        made = pltpu.make_async_copy(source, target, local_sem.at[number])
        made.start()
        loading.append(made)

    loading[0].wait()
    ids = jnp.minimum(near[...], 255)
    in_y, in_zh, in_x, low = ids >> 6, (ids >> 5) & 1, (ids >> 3) & 3, ids & 7
    by_row = in_zh * 32 + in_x * 8 + low + 64 * in_y
    by_col = in_zh * 32 + in_y * 8 + low + 64 * in_x
    role = jnp.zeros_like(ids) + core
    table[across, core] = jnp.zeros((8, 128), jnp.int32)
    table[across, core, 0:4, 0:8] = jnp.where(role == 0, by_row, by_col)
    table_out[...] = jnp.zeros((8, 128), jnp.int32)
    table_out[0:4, 0:8] = jnp.where(role == 0, by_col, by_row)

    for tile in range(4):
        loading[2 + tile].wait()
        first_row = feat[tile, 0]
        last_row = feat[tile, 31]
        for half in range(2):
            lanes = slice(half * 128, half * 128 + 128)
            wide[0:512, :] = feat[tile, :, 0:16, lanes].astype(F32).reshape(512, 128)
            wide[512:1024, :] = feat[tile, :, 16:32, lanes].astype(F32).reshape(512, 128)
            edges[0, half, tile, 0] = first_row[:, lanes]
            edges[0, half, tile, 1] = last_row[:, lanes]
            edges[1, half, tile, 0] = wide[pl.ds(0, 32, stride=16), :].astype(BF)
            edges[1, half, tile, 1] = wide[pl.ds(527, 32, stride=16), :].astype(BF)

    def block(plane, at):
        return pl.ds(pl.multiple_of(plane * 32 + at * 8, 8), 8)

    def part(plane, at, owner):
        return pl.ds(pl.multiple_of(plane * 32 + at * 8 + owner * 4, 4), 4)

    every[part(zh, along, core)] = edges[core, ch]
    for number in (8, 9, 10):
        loading[number].wait()

    pl.semaphore_wait(barrier, len(greeted))

    sent = []

    def copy(number, source, target, peer, arrives):
        return pltpu.make_async_remote_copy(
            src_ref=source,
            dst_ref=target,
            send_sem=send_sem.at[number],
            recv_sem=recv_sem.at[arrives],
            device_id=peer,
            device_id_type=MESH,
        )

    def start(number, source, target, peer, arrives):
        made = copy(number, source, target, peer, arrives)
        made.start()
        sent.append(made)

    def arrived(number, target):
        copy(0, target, target, sibling, number).wait_recv()

    def first_layer(tile):
        pre = dot(feat[tile].reshape(1024, 256), w1[...]) + b1[...]
        first_pre[tile] = pre
        act = pre * sigmoid(pre)
        padded[tile, 1:33, 8:40, :] = act.reshape(32, 32, 128)

    start(1, edges.at[1 - core, ch], every.at[part(zh, across, core)], sibling, 1)
    for k in range(2):
        start(
            2 + k,
            edges.at[k, 1 - ch],
            every.at[part(zh, x if k == 0 else y, core)],
            z_peers[k],
            2 + core,
        )
    start(0, table_out, table.at[along, core], sibling, 0)
    start(4, wm.at[0], wm.at[1], ch_same, 4)
    start(5, wl_part.at[0], wl_part.at[1], ch_same, 5)
    start(6, ws_part.at[0], ws_part.at[1], ch_same, 6)
    loading[6].wait()
    loading[7].wait()
    first_layer(0)

    arrived(1, every.at[part(zh, along, 1 - core)])
    own_block = every.at[block(zh, along)]
    start(7, own_block, own_block, gather_peer(1), 7)
    start(8, own_block, own_block, gather_peer(3), 8)
    arrived(0, table.at[across, 1 - core])
    for step in range(1, 4):
        start(8 + step, table.at[across], table.at[across], select_peer(step), 8 + step)
    arrived(2, every.at[part(1 - zh, along, 0)])
    arrived(3, every.at[part(1 - zh, along, 1)])
    far_block = every.at[block(1 - zh, along)]
    start(12, far_block, far_block, gather_peer(1), 12)
    start(13, far_block, far_block, gather_peer(3), 13)
    first_layer(1)
    before = lax.rem(along + 3, 4)
    after = lax.rem(along + 1, 4)
    opposite = lax.rem(along + 2, 4)
    for plane, first, second in ((zh, 7, 14), (1 - zh, 12, 16)):
        arrived(first, every.at[block(plane, before)])
        passed = every.at[part(plane, before, 0)]
        start(second, passed, passed, gather_peer(1), second)
        arrived(first + 1, every.at[block(plane, after)])
        passed = every.at[part(plane, after, 1)]
        start(second + 1, passed, passed, gather_peer(3), second + 1)
    for step in range(1, 4):
        arrived(8 + step, table.at[lax.rem(across + 4 - step, 4)])
    to_scalars = pltpu.make_async_copy(table, table_s, local_sem.at[len(loads)])
    to_scalars.start()
    first_layer(2)
    to_scalars.wait()
    for second, plane in ((14, zh), (16, 1 - zh)):
        arrived(second, every.at[part(plane, opposite, 0)])
        arrived(second + 1, every.at[part(plane, opposite, 1)])

    first_dir = 1 + 2 * core
    second_dir = 6 - 2 * core
    rows16 = lax.broadcasted_iota(jnp.int32, (16, 128), 0)

    for step in (2, 1, 3, 0):
        wanted = lax.rem(across + step, 4)
        into = pack.at[step] if step else got.at[0]

        def pack_tile(number, carry, wanted=wanted, into=into):
            owner, tile = number // 4, number % 4

            def held(d):
                return table_s[wanted, owner, tile, d] & 63

            into[owner, tile, 0:32, :] = every[held(first_dir), 1]
            into[owner, tile, 32:64, :] = every[held(second_dir), 0]
            corners = jnp.zeros((16, 128), F32)
            for k, (d, which, at) in enumerate(((0, 1, 31), (2, 1, 0), (5, 0, 31), (7, 0, 0))):
                near_rows = every[held(d), which, 16 * (at // 16) : 16 * (at // 16) + 16, :]
                near_rows = near_rows.astype(F32)[at % 16 : at % 16 + 1]
                corners = jnp.where(rows16 == k, near_rows, corners)
            into[owner, tile, 64:80, :] = corners.astype(BF)
            return carry

        lax.fori_loop(0, 8, pack_tile, 0)
        if step:
            start(17 + step, pack.at[step], got.at[step], select_peer(step), 17 + step)
    first_layer(3)
    for step in range(1, 4):
        arrived(17 + step, got.at[step])

    def finish_tile(owner, tile):
        def chosen(d, rows):
            from_step = (across + 4 - (table_s[across, owner, tile, d] >> 6)) & 3
            return got[from_step, owner, tile, rows, :]

        piece[owner, tile, 0:32, :] = chosen(first_dir, slice(0, 32))
        piece[owner, tile, 32:64, :] = chosen(second_dir, slice(32, 64))
        corners = jnp.zeros((16, 128), F32)
        for k, d in enumerate((0, 2, 5, 7)):
            corners = jnp.where(rows16 == k, chosen(d, slice(64, 80)).astype(F32), corners)
        piece[owner, tile, 64:80, :] = corners.astype(BF)

    for owner, copies in (
        (1 - core, ((23, ch_cross), (21, sibling))),
        (core, ((22, ch_same),)),
    ):
        lax.fori_loop(0, 4, lambda tile, c, owner=owner: (finish_tile(owner, tile), c)[1], 0)
        for number, peer in copies:
            start(number, piece.at[owner], halo.at[core, ch], peer, number)
    halo[core, ch] = piece[core]

    arrived(4, wm.at[1])
    arrived(5, wl_part.at[1])
    arrived(6, ws_part.at[1])
    for number in (11, 12):
        loading[number].wait()
    for i in range(3):
        for half in range(2):
            at = i * 128 + half * 64
            for j in range(3):
                source = (i * 3 + j) * 64
                wbt[at : at + 64, j * 128 : j * 128 + 128] = wm[half, source : source + 64, :]
        wf[i] = wbt[i * 128 : i * 128 + 128, :].astype(F32).T.astype(BF)
    own128 = pl.multiple_of(ch * 128, 128)
    other128 = pl.multiple_of((1 - ch) * 128, 128)
    wl[0:64, :] = wl_part[0]
    wl[64:128, :] = wl_part[1]
    ws[pl.ds(own128, 128), :] = ws_part[0]
    ws[pl.ds(other128, 128), :] = ws_part[1]
    bias = mid_bias_n[...]
    swapped = jnp.concatenate([bias[:, 64:128], bias[:, 0:64]], axis=1)
    mid_bias[...] = jnp.where(ch == 0, bias, swapped)
    for ref in (g_first, g_mid, g_last, g_side, g_first_bias, g_mid_bias, g_last_bias):
        ref[...] = jnp.zeros_like(ref)
    blank = jnp.zeros((32, 128), BF)
    for line, lanes in ((32, 0), (33, 0), (0, 128), (33, 128), (0, 256), (1, 256)):
        mid_delta[line, :, lanes : lanes + 128] = blank

    loading[1].wait()
    arrived(21, halo.at[1 - core, ch])
    arrived(22, halo.at[core, 1 - ch])
    arrived(23, halo.at[1 - core, 1 - ch])


    def here(tile, direction):
        return jnp.where(near_s[tile, direction] < 256, 1.0, 0.0).astype(F32)

    def rim_features(tile):
        return jnp.concatenate(
            [
                jnp.concatenate([halo[0, 0, tile], halo[0, 1, tile]], axis=1),
                jnp.concatenate([halo[1, 0, tile], halo[1, 1, tile]], axis=1),
            ],
            axis=0,
        )

    def pad(tile):
        pre = dot(rim_features(tile), w1[...]) + b1[...]
        rim_pre[...] = pre
        act = pre * sigmoid(pre)
        rim[...] = act
        padded[tile, 0, 8:40, :] = act[0:32] * here(tile, 1)
        padded[tile, 33, 8:40, :] = act[32:64] * here(tile, 6)
        padded[tile, 1:33, 7:8, :] = (act[80:112] * here(tile, 3)).reshape(32, 1, 128)
        padded[tile, 1:33, 40:41, :] = (act[112:144] * here(tile, 4)).reshape(32, 1, 128)
        padded[tile, 0, 7:8, :] = rim[64:65, :] * here(tile, 0)
        padded[tile, 0, 40:41, :] = rim[65:66, :] * here(tile, 2)
        padded[tile, 33, 7:8, :] = rim[66:67, :] * here(tile, 5)
        padded[tile, 33, 40:41, :] = rim[67:68, :] * here(tile, 7)
        for j in range(3):
            patches[:, :, j * 128 : j * 128 + 128] = padded[tile, :, 7 + j : 39 + j, :].astype(BF)

    high = CHUNK // 32

    def forward(tile, number):
        row = pl.multiple_of(number * CHUNK, CHUNK)
        line = number * high
        views = [patches[pl.ds(line + i, high)].reshape(CHUNK, 384) for i in range(3)]
        mid_pre = mid_bias[...] + dot(views[0], wf[0]) + dot(views[1], wf[1]) + dot(views[2], wf[2])
        mid_sig = sigmoid(mid_pre)
        mid_val = mid_pre * mid_sig
        mid_act = mid_val.astype(BF)
        x_part = feat[tile, pl.ds(line, high)].reshape(CHUNK, 256)
        out_pre = dot(mid_act, wl[...]) + dot(x_part, ws[...]) + last_bias[...]
        sig = sigmoid(out_pre)
        val = out_pre * sig
        out[tile, pl.ds(row, CHUNK), :] = val.astype(BF)
        return row, line, views, mid_sig, mid_val, mid_act, x_part, sig, val

    def write_out(tile, number):
        return pltpu.make_async_copy(out.at[tile], output.at[tile], out_sem.at[number])

    def forward_tile(tile, first, last):
        def body(number, carry):
            forward(tile, number)
            return carry

        lax.fori_loop(first, last, body, 0, unroll=True)

    def whole_tile(k, carry):
        tile = 2 * ch + k
        pad(tile)

        def body(number, inner):
            row, line, views, mid_sig, mid_val, mid_act, x_part, sig, val = forward(tile, number)
            slope = sig + val * (1.0 - sig)
            grad_out = (cot[k, pl.ds(row, CHUNK), :].astype(F32) * scale * slope).astype(BF)
            g_last[...] += dot_tn(mid_act, grad_out)
            g_side[...] += dot_tn(x_part, grad_out)
            g_last_bias[...] += grad_out.astype(F32).reshape(CHUNK // 8, 8, 512).sum(axis=0)
            mid_back = dot_nt(grad_out, wl[...])
            delta = (mid_back * (mid_sig + mid_val * (1.0 - mid_sig))).astype(BF)
            g_mid_bias[...] += delta.astype(F32).reshape(CHUNK // 8, 8, 128).sum(axis=0)
            for i in range(3):
                g_mid[i] += dot_tn(delta, views[i])
            for i in range(3):
                mid_delta[pl.ds(line + i, high), :, i * 128 : i * 128 + 128] = delta.reshape(
                    high, 32, 128
                )
            return inner

        lax.fori_loop(0, 1024 // CHUNK, body, 0, unroll=True)
        write_out(tile, k).start()

        back = dot(mid_delta[...].reshape(1088, 384), wbt[...]).reshape(34, 32, 384)
        spread[:, 0:8, :] = jnp.zeros((34, 8, 128), F32)
        spread[:, 40:48, :] = jnp.zeros((34, 8, 128), F32)
        spread[:, 8:40, :] = back[:, :, 128:256]
        spread[:, 7:39, :] += back[:, :, 0:128]
        spread[:, 9:41, :] += back[:, :, 256:384]

        pre = first_pre[tile]
        sig = sigmoid(pre)
        slope = sig + pre * sig * (1.0 - sig)
        delta = (spread[1:33, 8:40, :].reshape(1024, 128) * slope).astype(BF)
        rim[...] = jnp.zeros_like(rim)
        rim[0:32, :] = spread[0, 8:40, :] * here(tile, 1)
        rim[32:64, :] = spread[33, 8:40, :] * here(tile, 6)
        rim[64:65, :] = spread[0, 7:8, :] * here(tile, 0)
        rim[65:66, :] = spread[0, 40:41, :] * here(tile, 2)
        rim[66:67, :] = spread[33, 7:8, :] * here(tile, 5)
        rim[67:68, :] = spread[33, 40:41, :] * here(tile, 7)
        rim[80:112, :] = spread[1:33, 7:8, :].reshape(32, 128) * here(tile, 3)
        rim[112:144, :] = spread[1:33, 40:41, :].reshape(32, 128) * here(tile, 4)
        pre = rim_pre[...]
        sig = sigmoid(pre)
        slope = sig + pre * sig * (1.0 - sig)
        delta_rim = (rim[...] * slope).astype(BF)
        g_first[...] += dot_tn(delta, feat[tile].reshape(1024, 256))
        g_first[...] += dot_tn(delta_rim, rim_features(tile))
        g_first_bias[...] += delta.astype(F32).reshape(128, 8, 128).sum(axis=0)
        g_first_bias[...] += delta_rim.astype(F32).reshape(20, 8, 128).sum(axis=0)
        return carry

    loading[13].wait()
    loading[14].wait()
    lax.fori_loop(0, 2, whole_tile, 0)


    bias_first = jnp.sum(g_first_bias[...], axis=0, keepdims=True)
    bias_mid = jnp.sum(g_mid_bias[...], axis=0, keepdims=True)
    bias_last = jnp.sum(g_last_bias[...], axis=0, keepdims=True)
    for half in range(2):
        whose = ch if half == 0 else 1 - ch
        start64 = pl.multiple_of(whose * 64, 64)
        start128 = pl.multiple_of(whose * 128, 128)
        order = slice(half * 64, half * 64 + 64)
        for k in range(2):
            at = ROW_FIRST + k * 64
            lanes = slice(k * 128, k * 128 + 128)
            grads[half, at : at + 64, :] = g_first[pl.ds(start64, 64), lanes].astype(BF)
        for i in range(3):
            for j in range(3):
                at = ROW_MID + (i * 3 + j) * 64
                lanes = slice(j * 128, j * 128 + 128)
                grads[half, at : at + 64, :] = g_mid[i, order, lanes].astype(BF)
        for k in range(4):
            lanes = slice(k * 128, k * 128 + 128)
            at = ROW_LAST + k * 64
            grads[half, at : at + 64, :] = g_last[order, lanes].astype(BF)
            at = ROW_SIDE + k * 128
            grads[half, at : at + 128, :] = g_side[pl.ds(start128, 128), lanes].astype(BF)
        mid_row = bias_mid
        if half == 1:
            mid_row = jnp.concatenate([bias_mid[:, 64:128], bias_mid[:, 0:64]], axis=1)
        rows = jnp.where(rows16 == 0, bias_first, jnp.where(rows16 == 1, mid_row, 0.0))
        for k in range(4):
            rows = jnp.where(rows16 == 2 + k, bias_last[:, k * 128 : k * 128 + 128], rows)
        grads[half, ROW_BIAS : ROW_BIAS + 16, :] = rows.astype(BF)
        grads[half, ROW_BIAS + 16 : ROWS, :] = jnp.zeros((ROWS - ROW_BIAS - 16, 128), BF)


    def hand(number, source, target, peer):
        made = pltpu.make_async_remote_copy(
            src_ref=source,
            dst_ref=target,
            send_sem=sum_send_sem.at[number],
            recv_sem=sum_recv_sem.at[number],
            device_id=peer,
            device_id_type=MESH,
        )
        made.start()
        sent.append(made)
        return made

    third = lax.rem(2 + 2 * ch, 4)
    fourth = lax.rem(3 + 2 * ch, 4)
    count = 1024 // CHUNK

    own_rows = pl.multiple_of(core * CORE_ROWS, CORE_ROWS)
    other_rows = pl.multiple_of((1 - core) * CORE_ROWS, CORE_ROWS)
    swap = hand(0, grads.at[:, pl.ds(other_rows, CORE_ROWS)], from_core, sibling)
    pad(third)
    swap.wait_recv()
    for half in range(2):
        added = grads[half, pl.ds(own_rows, CORE_ROWS), :].astype(F32) + from_core[half].astype(F32)
        by_piece[:, half] = added.astype(BF).reshape(16, PIECE, 128)
    plane = []
    for step in range(1, 16):
        to = lax.rem(own_place + step, 16)
        plane.append(hand(step, by_piece.at[to], from_plane.at[step], plane_peer(step)))
    forward_tile(third, 0, count)
    write_out(third, 2).start()
    added = by_piece[own_place].astype(F32)
    for step, made in enumerate(plane, 1):
        made.wait_recv()
        added = added + from_plane[step].astype(F32)
    mine[...] = added.astype(BF)
    hops = []
    for k, (half, peer) in enumerate(((0, z_even), (1, ch_same), (1, z_odd))):
        hops.append(hand(16 + k, mine.at[half], from_z.at[k], peer))
    pad(fourth)
    forward_tile(fourth, 0, count // 2)
    added = added[0]
    for k, made in enumerate(hops):
        made.wait_recv()
        added = added + from_z[k].astype(F32)
    at = pl.multiple_of(own_rows + own_place * PIECE, 16)
    done[pl.ds(at, PIECE), :] = added.astype(BF)
    backs = []
    for step in range(1, 16):
        here_too = done.at[pl.ds(at, PIECE)]
        backs.append(hand(18 + step, here_too, here_too, plane_peer(step)))
    forward_tile(fourth, count // 2, count)
    write_out(fourth, 3).start()
    for made in backs:
        made.wait_recv()
    half_sum = done.at[pl.ds(own_rows, CORE_ROWS)]
    last = hand(34, half_sum, half_sum, sibling)
    last.wait_recv()
    whole_sum = pltpu.make_async_copy(done, total, out_sem.at[4])
    whole_sum.start()
    for made in sent:
        made.wait_send()
    for number, tile in enumerate((2 * ch, 2 * ch + 1, third, fourth)):
        write_out(tile, number).wait()
    whole_sum.wait()


def block(
    features,
    cotangent,
    neighbours,
    w1,
    b1,
    wm,
    mid_bias,
    wl,
    ws,
    last_bias,
):
    scale = 1.0 / math.sqrt(4096)
    anywhere = pl.BlockSpec(memory_space=pl.ANY)

    def kernel(*refs):
        block_kernel(scale, *refs)

    return pl.pallas_call(
        kernel,
        in_specs=[anywhere] * 10,
        out_specs=(anywhere, anywhere),
        out_shape=(
            jax.ShapeDtypeStruct((4, 1024, 512), BF),
            jax.ShapeDtypeStruct((ROWS, 128), BF),
        ),
        scratch_shapes=[
            pltpu.VMEM((4, 32, 32, 256), BF),
            pltpu.VMEM((2, 1024, 512), BF),
            pltpu.VMEM((4, 8), jnp.int32),
            pltpu.SMEM((4, 8), jnp.int32),
            pltpu.VMEM((256, 128), BF),
            pltpu.VMEM((1, 128), F32),
            pltpu.VMEM((2, 576, 128), BF),
            pltpu.VMEM((1, 128), F32),
            pltpu.VMEM((2, 64, 512), BF),
            pltpu.VMEM((2, 128, 512), BF),
            pltpu.VMEM((1, 512), F32),
            pltpu.VMEM((1024, 128), F32),
            pltpu.VMEM((2, 2, 4, 2, 32, 128), BF),
            pltpu.VMEM((4, 2, 8, 128), jnp.int32),
            pltpu.VMEM((8, 128), jnp.int32),
            pltpu.SMEM((4, 2, 8, 128), jnp.int32),
            pltpu.VMEM((64, 2, 32, 128), BF),
            pltpu.VMEM((4, 2, 4, 80, 128), BF),
            pltpu.VMEM((4, 2, 4, 80, 128), BF),
            pltpu.VMEM((2, 4, 80, 128), BF),
            pltpu.VMEM((2, 2, 4, 80, 128), BF),
            pltpu.VMEM((1, 128), F32),
            pltpu.VMEM((3, 384, 128), BF),
            pltpu.VMEM((384, 384), BF),
            pltpu.VMEM((128, 512), BF),
            pltpu.VMEM((256, 512), BF),
            pltpu.VMEM((4, 1024, 128), F32),
            pltpu.VMEM((160, 128), F32),
            pltpu.VMEM((4, 34, 48, 128), F32),
            pltpu.VMEM((34, 32, 384), BF),
            pltpu.VMEM((34, 32, 384), BF),
            pltpu.VMEM((34, 48, 128), F32),
            pltpu.VMEM((160, 128), F32),
            pltpu.VMEM((4, 1024, 512), BF),
            pltpu.VMEM((128, 256), F32),
            pltpu.VMEM((3, 128, 384), F32),
            pltpu.VMEM((128, 512), F32),
            pltpu.VMEM((256, 512), F32),
            pltpu.VMEM((8, 128), F32),
            pltpu.VMEM((8, 128), F32),
            pltpu.VMEM((8, 512), F32),
            pltpu.VMEM((2, ROWS, 128), BF),
            pltpu.VMEM((2, CORE_ROWS, 128), BF),
            pltpu.VMEM((16, 2, PIECE, 128), BF),
            pltpu.VMEM((16, 2, PIECE, 128), BF),
            pltpu.VMEM((2, PIECE, 128), BF),
            pltpu.VMEM((3, PIECE, 128), BF),
            pltpu.VMEM((ROWS, 128), BF),
            pltpu.SemaphoreType.DMA((16,)),
            pltpu.SemaphoreType.DMA((5,)),
            pltpu.SemaphoreType.DMA((24,)),
            pltpu.SemaphoreType.DMA((24,)),
            pltpu.SemaphoreType.DMA((35,)),
            pltpu.SemaphoreType.DMA((35,)),
        ],
        compiler_params=pltpu.CompilerParams(
            collective_id=0, has_side_effects=True, vmem_limit_bytes=60 * 2**20
        ),
    )(features, cotangent, neighbours, w1, b1, wm, mid_bias, wl, ws, last_bias)


def finish_kernel(
    out,
    total_h,
    output,
    g_first,
    g_first_bias,
    g_mid,
    g_mid_bias,
    g_last,
    g_side,
    g_last_bias,
    total,
    staged,
    in_sem,
    out_sem,
):
    loading = pltpu.make_async_copy(total_h, total, in_sem.at[PARTS])
    loading.start()
    reads, writes = [], []
    for k in range(PARTS):
        reads.append(pltpu.make_async_copy(out.at[k], staged.at[k], in_sem.at[k]))
        writes.append(pltpu.make_async_copy(staged.at[k], output.at[k], out_sem.at[k]))
        reads[k].start()
    for k in range(PARTS):
        reads[k].wait()
        writes[k].start()
    loading.wait()

    def rows(at, count):
        return total[at : at + count, :].astype(F32)

    for k in range(2):
        g_first[:, k * 128 : k * 128 + 128] = rows(ROW_FIRST + k * 64, 64)
    for k in range(9):
        g_mid[k // 3, k % 3] = rows(ROW_MID + k * 64, 64)
    bias = rows(ROW_BIAS, 16)
    for k in range(4):
        lanes = slice(k * 128, k * 128 + 128)
        g_last[:, lanes] = rows(ROW_LAST + k * 64, 64)
        g_side[:, lanes] = rows(ROW_SIDE + k * 128, 128)
        g_last_bias[:, lanes] = bias[2 + k : 3 + k, :]
    ch = lax.axis_index("ch")
    g_first_bias[...] = jnp.where(ch == 0, bias[0:1, 0:64], bias[0:1, 64:128])
    g_mid_bias[...] = bias[1:2, 0:64]
    for made in writes:
        made.wait()


def finish(out, total):
    vmem = pl.BlockSpec(memory_space=pltpu.VMEM)
    return pl.pallas_call(
        finish_kernel,
        in_specs=[pl.BlockSpec(memory_space=pl.ANY)] * 2,
        out_specs=(pl.BlockSpec(memory_space=pl.ANY), *[vmem] * 7),
        out_shape=(
            jax.ShapeDtypeStruct(out.shape, BF),
            *[
                jax.ShapeDtypeStruct(shape, F32)
                for shape in (
                    (64, 256),
                    (1, 64),
                    (3, 3, 64, 128),
                    (1, 64),
                    (64, 512),
                    (128, 512),
                    (1, 512),
                )
            ],
        ),
        scratch_shapes=[
            pltpu.VMEM((ROWS, 128), BF),
            pltpu.VMEM(out.shape, BF),
            pltpu.SemaphoreType.DMA((PARTS + 1,)),
            pltpu.SemaphoreType.DMA((PARTS,)),
        ],
        compiler_params=pltpu.CompilerParams(vmem_limit_bytes=60 * 2**20),
    )(out, total)


def per_device(
    features,
    cotangent,
    neighbours,
    first_weight,
    first_bias,
    mid_weight,
    mid_bias,
    last_weight,
    side_weight,
    last_bias,
):
    out, total = block(
        features,
        cotangent.reshape(4096, 512),
        neighbours,
        first_weight,
        first_bias.reshape(1, 128),
        mid_weight.transpose(0, 1, 3, 2).reshape(576, 128),
        mid_bias.reshape(1, 128),
        last_weight,
        side_weight,
        last_bias.reshape(1, 512),
    )
    output, g_first, g_first_bias, g_mid, g_mid_bias, g_last, g_side, g_last_bias = finish(
        out.reshape(PARTS, 4096 // PARTS, 512), total
    )
    return (
        output.reshape(4, 32, 32, 512),
        g_first.T,
        g_first_bias.reshape(64),
        g_mid.transpose(0, 1, 3, 2),
        g_mid_bias.reshape(64),
        g_last,
        g_side,
        g_last_bias.reshape(512),
    )


def solution(mesh):
    return jax.shard_map(
        per_device,
        mesh=mesh,
        in_specs=(
            P("tile", None, None, None),
            P("tile", None, None, None),
            P("tile", None),
            P(),
            P(),
            P(None, None, None, "ch"),
            P(),
            P("ch", None),
            P("ch", None),
            P(),
        ),
        out_specs=(
            P("tile", None, None, None),
            P(None, "ch"),
            P("ch"),
            P(None, None, None, "ch"),
            P("ch"),
            P("ch", None),
            P("ch", None),
            P(),
        ),
        check_vma=False,
    )
```

```python
import math

import jax
import jax.numpy as jnp
from jax import lax
from jax.experimental import pallas as pl
from jax.experimental.pallas import tpu as pltpu
from jax.sharding import PartitionSpec as P

BF = jnp.bfloat16
F32 = jnp.float32
MESH = pl.DeviceIdType.MESH

ROW_FIRST = 0
ROW_MID = 128
ROW_LAST = 704
ROW_SIDE = 960
ROW_BIAS = 1472
ROWS = 1536
CORE_ROWS = ROWS // 2
PIECE = CORE_ROWS // 16

CORNERS = ((0, 1, 31), (2, 1, 0), (5, 0, 31), (7, 0, 0))
PLACES = ((0, 0, 7), (2, 0, 40), (5, 33, 7), (7, 33, 40))

CHUNK = 512
PARTS = 8


def place():
    tile = lax.axis_index("tile")
    ch = lax.axis_index("ch")
    return tile // 16, (tile // 8) % 2, (tile // 2) % 4, tile % 2, ch


def device(y, zh, x, core, ch):
    return (((y * 2 + zh) * 4 + x) * 2 + core, ch)


def sigmoid(v):
    return 0.5 + 0.5 * jnp.tanh(0.5 * v)


def dot(a, b):
    return jnp.dot(a, b, preferred_element_type=F32)


def dot_nt(a, b):
    return lax.dot_general(a, b, (((1,), (1,)), ((), ())), preferred_element_type=F32)


def dot_tn(a, b):
    return lax.dot_general(a, b, (((0,), (0,)), ((), ())), preferred_element_type=F32)


def block_kernel(
    scale,
    features,
    cotangent,
    neighbours,
    w1_h,
    b1_h,
    wm_h,
    mid_bias_h,
    wl_h,
    ws_h,
    last_bias_h,
    out,
    total,
    feat,
    cot,
    near,
    near_s,
    w1,
    b1,
    wm,
    mid_bias_n,
    wl_part,
    ws_part,
    last_bias,
    wide,
    edges,
    table,
    table_out,
    table_s,
    every,
    pack,
    got_first,
    got_second,
    piece,
    halo,
    mid_bias,
    wf,
    wbt,
    wl,
    ws,
    first_pre,
    rim_pre,
    padded,
    patches,
    mid_delta,
    spread,
    rim,
    g_first,
    g_mid,
    g_last,
    g_side,
    g_first_bias,
    g_mid_bias,
    g_last_bias,
    grads,
    from_core,
    by_piece,
    from_plane,
    mine,
    from_z,
    done,
    local_sem,
    send_sem,
    recv_sem,
    sum_send_sem,
    sum_recv_sem,
):
    y, zh, x, core, ch = place()
    row_role = core == 0
    along = jnp.where(row_role, x, y)
    across = jnp.where(row_role, y, x)
    own_place = y * 4 + x

    def gather_peer(step):
        to = lax.rem(along + step, 4)
        return device(jnp.where(row_role, y, to), zh, jnp.where(row_role, to, x), core, ch)

    def select_peer(step):
        to = lax.rem(across + step, 4)
        return device(jnp.where(row_role, to, y), zh, jnp.where(row_role, x, to), core, ch)

    def plane_peer(step):
        to = lax.rem(own_place + step, 16)
        return device(to // 4, zh, to % 4, core, ch)

    sibling = device(y, zh, x, 1 - core, ch)
    z_peers = [device(y, 1 - zh, x, role, 1 - ch) for role in (0, 1)]
    ch_same = device(y, zh, x, core, 1 - ch)
    ch_cross = device(y, zh, x, 1 - core, 1 - ch)
    z_even = device(y, 1 - zh, x, core, ch)
    z_odd = device(y, 1 - zh, x, core, 1 - ch)

    barrier = pltpu.get_barrier_semaphore()
    greeted = [sibling, *z_peers, ch_same, ch_cross, z_even]
    greeted += [plane_peer(step) for step in range(1, 16)]
    for peer in greeted:
        pl.semaphore_signal(barrier, inc=1, device_id=peer, device_id_type=MESH)

    loads = [
        (neighbours, near),
        (neighbours, near_s),
        *[(features.at[tile], feat.at[tile]) for tile in range(4)],
        (w1_h, w1),
        (b1_h, b1),
        (wm_h, wm.at[0]),
        (wl_h, wl_part.at[0]),
        (ws_h, ws_part.at[0]),
        (mid_bias_h, mid_bias_n),
        (last_bias_h, last_bias),
    ]
    loads += [
        (cotangent.at[pl.ds(pl.multiple_of((2 * ch + k) * 1024, 1024), 1024)], cot.at[k])
        for k in range(2)
    ]
    loading = []
    for number, (source, target) in enumerate(loads):
        made = pltpu.make_async_copy(source, target, local_sem.at[number])
        made.start()
        loading.append(made)

    loading[0].wait()
    ids = jnp.minimum(near[...], 255)
    in_y, in_zh, in_x, low = ids >> 6, (ids >> 5) & 1, (ids >> 3) & 3, ids & 7
    by_row = in_zh * 32 + in_x * 8 + low + 64 * in_y
    by_col = in_zh * 32 + in_y * 8 + low + 64 * in_x
    role = jnp.zeros_like(ids) + core
    table[across, core] = jnp.zeros((8, 128), jnp.int32)
    table[across, core, 0:4, 0:8] = jnp.where(role == 0, by_row, by_col)
    table_out[...] = jnp.zeros((8, 128), jnp.int32)
    table_out[0:4, 0:8] = jnp.where(role == 0, by_col, by_row)

    for tile in range(4):
        loading[2 + tile].wait()
        first_row = feat[tile, 0]
        last_row = feat[tile, 31]
        for half in range(2):
            lanes = slice(half * 128, half * 128 + 128)
            wide[0:512, :] = feat[tile, :, 0:16, lanes].astype(F32).reshape(512, 128)
            wide[512:1024, :] = feat[tile, :, 16:32, lanes].astype(F32).reshape(512, 128)
            edges[0, half, tile, 0] = first_row[:, lanes]
            edges[0, half, tile, 1] = last_row[:, lanes]
            edges[1, half, tile, 0] = wide[pl.ds(0, 32, stride=16), :].astype(BF)
            edges[1, half, tile, 1] = wide[pl.ds(527, 32, stride=16), :].astype(BF)

    def part(plane, at, owner):
        return pl.ds(pl.multiple_of(plane * 32 + at * 8 + owner * 4, 4), 4)

    every[part(zh, along, core)] = edges[core, ch]
    for number in (8, 9, 10):
        loading[number].wait()

    pl.semaphore_wait(barrier, len(greeted))

    sent = []

    def copy(number, source, target, peer, arrives):
        return pltpu.make_async_remote_copy(
            src_ref=source,
            dst_ref=target,
            send_sem=send_sem.at[number],
            recv_sem=recv_sem.at[arrives],
            device_id=peer,
            device_id_type=MESH,
        )

    def start(number, source, target, peer, arrives):
        made = copy(number, source, target, peer, arrives)
        made.start()
        sent.append(made)

    def arrived(number, target):
        copy(0, target, target, sibling, number).wait_recv()

    def first_layer(tile):
        pre = dot(feat[tile].reshape(1024, 256), w1[...]) + b1[...]
        first_pre[tile] = pre
        act = pre * sigmoid(pre)
        padded[tile, 1:33, 8:40, :] = act.reshape(32, 32, 128)

    start(1, edges.at[1 - core, ch], every.at[part(zh, across, core)], sibling, 1)
    for k in range(2):
        start(
            2 + k,
            edges.at[k, 1 - ch],
            every.at[part(zh, x if k == 0 else y, core)],
            z_peers[k],
            2 + core,
        )
    def ring_number(far, owner, back):
        return 30 + far * 4 + owner * 2 + back

    def ring(far, owner):
        strips = every.at[part(1 - zh if far else zh, along, owner)]
        for back, peer in ((0, gather_peer(1)), (1, gather_peer(3))):
            number = ring_number(far, owner, back)
            start(number, strips, strips, peer, number)

    ring(0, core)
    start(0, table_out, table.at[along, core], sibling, 0)
    start(4, wm.at[0], wm.at[1], ch_same, 4)
    start(5, wl_part.at[0], wl_part.at[1], ch_same, 5)
    start(6, ws_part.at[0], ws_part.at[1], ch_same, 6)
    loading[6].wait()
    loading[7].wait()
    first_layer(0)

    arrived(1, every.at[part(zh, along, 1 - core)])
    ring(0, 1 - core)
    arrived(0, table.at[across, 1 - core])
    for step in range(1, 4):
        start(8 + step, table.at[across], table.at[across], select_peer(step), 8 + step)
    for owner in range(2):
        arrived(2 + owner, every.at[part(1 - zh, along, owner)])
        ring(1, owner)
    first_layer(1)
    before = lax.rem(along + 3, 4)
    after = lax.rem(along + 1, 4)
    opposite = lax.rem(along + 2, 4)
    for far, plane in enumerate((zh, 1 - zh)):
        for owner, back, origin, peer in (
            (0, 0, before, gather_peer(1)),
            (1, 1, after, gather_peer(3)),
        ):
            passed = every.at[part(plane, origin, owner)]
            arrived(ring_number(far, owner, back), passed)
            start(14 + far * 2 + owner, passed, passed, peer, 14 + far * 2 + owner)
    for step in range(1, 4):
        arrived(8 + step, table.at[lax.rem(across + 4 - step, 4)])
    to_scalars = pltpu.make_async_copy(table, table_s, local_sem.at[len(loads)])
    to_scalars.start()
    first_layer(2)
    arrived(4, wm.at[1])
    arrived(5, wl_part.at[1])
    arrived(6, ws_part.at[1])
    for number in (11, 12):
        loading[number].wait()
    for i in range(3):
        for half in range(2):
            at = i * 128 + half * 64
            for j in range(3):
                source = (i * 3 + j) * 64
                wbt[at : at + 64, j * 128 : j * 128 + 128] = wm[half, source : source + 64, :]
        wf[i] = wbt[i * 128 : i * 128 + 128, :].astype(F32).T.astype(BF)
    own128 = pl.multiple_of(ch * 128, 128)
    other128 = pl.multiple_of((1 - ch) * 128, 128)
    wl[0:64, :] = wl_part[0]
    wl[64:128, :] = wl_part[1]
    ws[pl.ds(own128, 128), :] = ws_part[0]
    ws[pl.ds(other128, 128), :] = ws_part[1]
    bias = mid_bias_n[...]
    swapped = jnp.concatenate([bias[:, 64:128], bias[:, 0:64]], axis=1)
    mid_bias[...] = jnp.where(ch == 0, bias, swapped)
    for ref in (g_first, g_mid, g_last, g_side, g_first_bias, g_mid_bias, g_last_bias):
        ref[...] = jnp.zeros_like(ref)
    blank = jnp.zeros((32, 128), BF)
    for line, lanes in ((32, 0), (33, 0), (0, 128), (33, 128), (0, 256), (1, 256)):
        mid_delta[line, :, lanes : lanes + 128] = blank
    to_scalars.wait()
    for far, plane in enumerate((zh, 1 - zh)):
        arrived(ring_number(far, 1, 0), every.at[part(plane, before, 1)])
        arrived(ring_number(far, 0, 1), every.at[part(plane, after, 0)])
        arrived(14 + far * 2, every.at[part(plane, opposite, 0)])
        arrived(15 + far * 2, every.at[part(plane, opposite, 1)])

    first_dir = 1 + 2 * core
    second_dir = 6 - 2 * core
    rows16 = lax.broadcasted_iota(jnp.int32, (16, 128), 0)

    got = (got_first, got_second)

    def pack_round(step, turn):
        wanted = lax.rem(across + step, 4)
        into = pack.at[step, turn] if step else got[turn].at[0]

        def pack_tile(slot, corners):
            owner, tile = slot // 2, turn + 2 * (slot % 2)

            def held(d):
                return table_s[wanted, owner, tile, d] & 63

            at = slot * 64
            into[pl.ds(at, 32), :] = every[held(first_dir), 1]
            into[pl.ds(at + 32, 32), :] = every[held(second_dir), 0]
            for k, (d, which, line) in enumerate(CORNERS):
                rows = every[held(d), which, 16 * (line // 16) : 16 * (line // 16) + 16, :]
                row = rows.astype(F32)[line % 16 : line % 16 + 1]
                corners = jnp.where(rows16 == slot * 4 + k, row, corners)
            return corners

        corners = jnp.zeros((16, 128), F32)
        for slot in range(4):
            corners = pack_tile(slot, corners)
        into[256:272, :] = corners.astype(BF)
        if step:
            number = 17 + turn * 3 + step
            start(number, pack.at[step, turn], got[turn].at[step], select_peer(step), number)

    def finish_round(owner, turn):
        def finish_tile(k, corners):
            slot, tile = owner * 2 + k, turn + 2 * k

            def chosen(d, rows):
                from_step = (across + 4 - (table_s[across, owner, tile, d] >> 6)) & 3
                return got[turn][from_step, rows, :]

            at = pl.multiple_of(slot * 64, 64)
            to = k * 64
            piece[turn, owner, pl.ds(to, 32), :] = chosen(first_dir, pl.ds(at, 32))
            piece[turn, owner, pl.ds(to + 32, 32), :] = chosen(second_dir, pl.ds(at + 32, 32))
            for c, (d, _, _) in enumerate(CORNERS):
                rows = chosen(d, slice(256, 272)).astype(F32)
                corners = jnp.where(rows16 == slot * 4 + c, rows, corners)
            return corners

        corners = jnp.zeros((16, 128), F32)
        for k in range(2):
            corners = finish_tile(k, corners)
        half = jnp.where(owner == 0, corners[0:8], corners[8:16])
        both = jnp.concatenate([half, half], axis=0)
        piece[turn, owner, 128:144, :] = both.astype(BF)

    for turn in range(2):
        for step in (2, 1, 3):
            pack_round(step, turn)
    pack_round(0, 0)
    pack_round(0, 1)
    first_layer(3)
    for turn in range(2):
        for step in range(1, 4):
            arrived(17 + turn * 3 + step, got[turn].at[step])
        for owner, copies in (
            (1 - core, ((0, ch_cross), (1, sibling))),
            (core, ((2, ch_same),)),
        ):
            finish_round(owner, turn)
            for k, peer in copies:
                number = 24 + turn * 3 + k
                start(number, piece.at[turn, owner], halo.at[core, ch, turn], peer, number)
        halo[core, ch, turn] = piece[turn, core]

    def halo_arrived(turn):
        arrived(24 + turn * 3, halo.at[1 - core, 1 - ch, turn])
        arrived(25 + turn * 3, halo.at[1 - core, ch, turn])
        arrived(26 + turn * 3, halo.at[core, 1 - ch, turn])

    loading[1].wait()


    def here(tile, direction):
        return jnp.where(near_s[tile, direction] < 256, 1.0, 0.0).astype(F32)

    def rim_features(turn, which):
        rows = pl.ds(pl.multiple_of(which * 64, 64), 64)
        parts = [(0, rows), (1, rows), (0, slice(128, 144))]
        return jnp.concatenate(
            [jnp.concatenate([halo[r, h, turn, at, :] for h in range(2)], axis=1) for r, at in parts],
            axis=0,
        )

    def pad(tile, turn, which):
        pre = dot(rim_features(turn, which), w1[...]) + b1[...]
        rim_pre[...] = pre
        act = pre * sigmoid(pre)
        rim[...] = act
        padded[tile, 0, 8:40, :] = act[0:32] * here(tile, 1)
        padded[tile, 33, 8:40, :] = act[32:64] * here(tile, 6)
        padded[tile, 1:33, 7:8, :] = (act[64:96] * here(tile, 3)).reshape(32, 1, 128)
        padded[tile, 1:33, 40:41, :] = (act[96:128] * here(tile, 4)).reshape(32, 1, 128)
        for k, (d, line, column) in enumerate(PLACES):
            row = rim[pl.ds(128 + which * 4 + k, 1), :]
            padded[tile, line, column : column + 1, :] = row * here(tile, d)
        for j in range(3):
            patches[:, :, j * 128 : j * 128 + 128] = padded[tile, :, 7 + j : 39 + j, :].astype(BF)

    high = CHUNK // 32

    def forward(tile, number):
        row = pl.multiple_of(number * CHUNK, CHUNK)
        line = number * high
        views = [patches[pl.ds(line + i, high)].reshape(CHUNK, 384) for i in range(3)]
        mid_pre = mid_bias[...] + dot(views[0], wf[0]) + dot(views[1], wf[1]) + dot(views[2], wf[2])
        mid_sig = sigmoid(mid_pre)
        mid_val = mid_pre * mid_sig
        mid_act = mid_val.astype(BF)
        x_part = feat[tile, pl.ds(line, high)].reshape(CHUNK, 256)
        out_pre = dot(mid_act, wl[...]) + dot(x_part, ws[...]) + last_bias[...]
        sig = sigmoid(out_pre)
        val = out_pre * sig
        out[tile, pl.ds(row, CHUNK), :] = val.astype(BF)
        return row, line, views, mid_sig, mid_val, mid_act, x_part, sig, val

    def forward_tile(tile, first, last):
        def body(number, carry):
            forward(tile, number)
            return carry

        lax.fori_loop(first, last, body, 0, unroll=True)

    def whole_tile(k, carry):
        tile = 2 * ch + k
        halo_arrived(k)
        pad(tile, k, ch)

        def body(number, inner):
            row, line, views, mid_sig, mid_val, mid_act, x_part, sig, val = forward(tile, number)
            slope = sig + val * (1.0 - sig)
            grad_out = (cot[k, pl.ds(row, CHUNK), :].astype(F32) * scale * slope).astype(BF)
            g_last[...] += dot_tn(mid_act, grad_out)
            g_side[...] += dot_tn(x_part, grad_out)
            g_last_bias[...] += grad_out.astype(F32).reshape(CHUNK // 8, 8, 512).sum(axis=0)
            mid_back = dot_nt(grad_out, wl[...])
            delta = (mid_back * (mid_sig + mid_val * (1.0 - mid_sig))).astype(BF)
            g_mid_bias[...] += delta.astype(F32).reshape(CHUNK // 8, 8, 128).sum(axis=0)
            for i in range(3):
                g_mid[i] += dot_tn(delta, views[i])
            for i in range(3):
                mid_delta[pl.ds(line + i, high), :, i * 128 : i * 128 + 128] = delta.reshape(
                    high, 32, 128
                )
            return inner

        lax.fori_loop(0, 1024 // CHUNK, body, 0, unroll=True)

        back = dot(mid_delta[...].reshape(1088, 384), wbt[...]).reshape(34, 32, 384)
        spread[:, 0:8, :] = jnp.zeros((34, 8, 128), F32)
        spread[:, 40:48, :] = jnp.zeros((34, 8, 128), F32)
        spread[:, 8:40, :] = back[:, :, 128:256]
        spread[:, 7:39, :] += back[:, :, 0:128]
        spread[:, 9:41, :] += back[:, :, 256:384]

        pre = first_pre[tile]
        sig = sigmoid(pre)
        slope = sig + pre * sig * (1.0 - sig)
        delta = (spread[1:33, 8:40, :].reshape(1024, 128) * slope).astype(BF)
        rim[...] = jnp.zeros_like(rim)
        rim[0:32, :] = spread[0, 8:40, :] * here(tile, 1)
        rim[32:64, :] = spread[33, 8:40, :] * here(tile, 6)
        rim[64:96, :] = spread[1:33, 7:8, :].reshape(32, 128) * here(tile, 3)
        rim[96:128, :] = spread[1:33, 40:41, :].reshape(32, 128) * here(tile, 4)
        for c, (d, line, column) in enumerate(PLACES):
            row = spread[line, column : column + 1, :]
            rim[pl.ds(128 + ch * 4 + c, 1), :] = row * here(tile, d)
        pre = rim_pre[...]
        sig = sigmoid(pre)
        slope = sig + pre * sig * (1.0 - sig)
        delta_rim = (rim[...] * slope).astype(BF)
        g_first[...] += dot_tn(delta, feat[tile].reshape(1024, 256))
        g_first[...] += dot_tn(delta_rim, rim_features(k, ch))
        g_first_bias[...] += delta.astype(F32).reshape(128, 8, 128).sum(axis=0)
        g_first_bias[...] += delta_rim.astype(F32).reshape(18, 8, 128).sum(axis=0)
        return carry

    loading[13].wait()
    loading[14].wait()
    lax.fori_loop(0, 2, whole_tile, 0)


    bias_first = jnp.sum(g_first_bias[...], axis=0, keepdims=True)
    bias_mid = jnp.sum(g_mid_bias[...], axis=0, keepdims=True)
    bias_last = jnp.sum(g_last_bias[...], axis=0, keepdims=True)
    for half in range(2):
        whose = ch if half == 0 else 1 - ch
        start64 = pl.multiple_of(whose * 64, 64)
        start128 = pl.multiple_of(whose * 128, 128)
        order = slice(half * 64, half * 64 + 64)
        for k in range(2):
            at = ROW_FIRST + k * 64
            lanes = slice(k * 128, k * 128 + 128)
            grads[half, at : at + 64, :] = g_first[pl.ds(start64, 64), lanes].astype(BF)
        for i in range(3):
            for j in range(3):
                at = ROW_MID + (i * 3 + j) * 64
                lanes = slice(j * 128, j * 128 + 128)
                grads[half, at : at + 64, :] = g_mid[i, order, lanes].astype(BF)
        for k in range(4):
            lanes = slice(k * 128, k * 128 + 128)
            at = ROW_LAST + k * 64
            grads[half, at : at + 64, :] = g_last[order, lanes].astype(BF)
            at = ROW_SIDE + k * 128
            grads[half, at : at + 128, :] = g_side[pl.ds(start128, 128), lanes].astype(BF)
        mid_row = bias_mid
        if half == 1:
            mid_row = jnp.concatenate([bias_mid[:, 64:128], bias_mid[:, 0:64]], axis=1)
        rows = jnp.where(rows16 == 0, bias_first, jnp.where(rows16 == 1, mid_row, 0.0))
        for k in range(4):
            rows = jnp.where(rows16 == 2 + k, bias_last[:, k * 128 : k * 128 + 128], rows)
        grads[half, ROW_BIAS : ROW_BIAS + 16, :] = rows.astype(BF)
        grads[half, ROW_BIAS + 16 : ROWS, :] = jnp.zeros((ROWS - ROW_BIAS - 16, 128), BF)


    def hand(number, source, target, peer):
        made = pltpu.make_async_remote_copy(
            src_ref=source,
            dst_ref=target,
            send_sem=sum_send_sem.at[number],
            recv_sem=sum_recv_sem.at[number],
            device_id=peer,
            device_id_type=MESH,
        )
        made.start()
        sent.append(made)
        return made

    third = lax.rem(2 + 2 * ch, 4)
    fourth = lax.rem(3 + 2 * ch, 4)
    count = 1024 // CHUNK

    own_rows = pl.multiple_of(core * CORE_ROWS, CORE_ROWS)
    other_rows = pl.multiple_of((1 - core) * CORE_ROWS, CORE_ROWS)
    swap = hand(0, grads.at[:, pl.ds(other_rows, CORE_ROWS)], from_core, sibling)
    pad(third, 0, 1 - ch)
    swap.wait_recv()
    for half in range(2):
        added = grads[half, pl.ds(own_rows, CORE_ROWS), :].astype(F32) + from_core[half].astype(F32)
        by_piece[:, half] = added.astype(BF).reshape(16, PIECE, 128)
    plane = []
    for step in range(1, 16):
        to = lax.rem(own_place + step, 16)
        plane.append(hand(step, by_piece.at[to], from_plane.at[step], plane_peer(step)))
    forward_tile(third, 0, count)
    added = by_piece[own_place].astype(F32)
    for step, made in enumerate(plane, 1):
        made.wait_recv()
        added = added + from_plane[step].astype(F32)
    mine[...] = added.astype(BF)
    hops = []
    for k, (half, peer) in enumerate(((0, z_even), (1, ch_same), (1, z_odd))):
        hops.append(hand(16 + k, mine.at[half], from_z.at[k], peer))
    pad(fourth, 1, 1 - ch)
    forward_tile(fourth, 0, count // 2)
    added = added[0]
    for k, made in enumerate(hops):
        made.wait_recv()
        added = added + from_z[k].astype(F32)
    at = pl.multiple_of(own_rows + own_place * PIECE, 16)
    done[pl.ds(at, PIECE), :] = added.astype(BF)
    def cross(step):
        origin = lax.rem(own_place + 16 - step, 16)
        rows = done.at[pl.ds(pl.multiple_of(own_rows + origin * PIECE, 16), PIECE)]
        return hand(34 + step, rows, rows, sibling)

    backs, crossings = [], []
    for step in range(1, 16):
        here_too = done.at[pl.ds(at, PIECE)]
        backs.append(hand(18 + step, here_too, here_too, plane_peer(step)))
    crossings.append(cross(0))
    forward_tile(fourth, count // 2, count)
    for step, made in enumerate(backs, 1):
        made.wait_recv()
        crossings.append(cross(step))
    for made in crossings:
        made.wait_recv()
    total[...] = done[...]
    for made in sent:
        made.wait_send()


def block(*operands):
    scale = 1.0 / math.sqrt(4096)
    anywhere = pl.BlockSpec(memory_space=pl.ANY)

    def kernel(*refs):
        block_kernel(scale, *refs)

    return pl.pallas_call(
        kernel,
        in_specs=[anywhere] * 10,
        out_specs=(pl.BlockSpec(memory_space=pltpu.VMEM),) * 2,
        out_shape=(
            jax.ShapeDtypeStruct((4, 1024, 512), BF),
            jax.ShapeDtypeStruct((ROWS, 128), BF),
        ),
        scratch_shapes=[
            pltpu.VMEM((4, 32, 32, 256), BF),
            pltpu.VMEM((2, 1024, 512), BF),
            pltpu.VMEM((4, 8), jnp.int32),
            pltpu.SMEM((4, 8), jnp.int32),
            pltpu.VMEM((256, 128), BF),
            pltpu.VMEM((1, 128), F32),
            pltpu.VMEM((2, 576, 128), BF),
            pltpu.VMEM((1, 128), F32),
            pltpu.VMEM((2, 64, 512), BF),
            pltpu.VMEM((2, 128, 512), BF),
            pltpu.VMEM((1, 512), F32),
            pltpu.VMEM((1024, 128), F32),
            pltpu.VMEM((2, 2, 4, 2, 32, 128), BF),
            pltpu.VMEM((4, 2, 8, 128), jnp.int32),
            pltpu.VMEM((8, 128), jnp.int32),
            pltpu.SMEM((4, 2, 8, 128), jnp.int32),
            pltpu.VMEM((64, 2, 32, 128), BF),
            pltpu.VMEM((4, 2, 272, 128), BF),
            pltpu.VMEM((4, 272, 128), BF),
            pltpu.VMEM((4, 272, 128), BF),
            pltpu.VMEM((2, 2, 144, 128), BF),
            pltpu.VMEM((2, 2, 2, 144, 128), BF),
            pltpu.VMEM((1, 128), F32),
            pltpu.VMEM((3, 384, 128), BF),
            pltpu.VMEM((384, 384), BF),
            pltpu.VMEM((128, 512), BF),
            pltpu.VMEM((256, 512), BF),
            pltpu.VMEM((4, 1024, 128), F32),
            pltpu.VMEM((144, 128), F32),
            pltpu.VMEM((4, 34, 48, 128), F32),
            pltpu.VMEM((34, 32, 384), BF),
            pltpu.VMEM((34, 32, 384), BF),
            pltpu.VMEM((34, 48, 128), F32),
            pltpu.VMEM((144, 128), F32),
            pltpu.VMEM((128, 256), F32),
            pltpu.VMEM((3, 128, 384), F32),
            pltpu.VMEM((128, 512), F32),
            pltpu.VMEM((256, 512), F32),
            pltpu.VMEM((8, 128), F32),
            pltpu.VMEM((8, 128), F32),
            pltpu.VMEM((8, 512), F32),
            pltpu.VMEM((2, ROWS, 128), BF),
            pltpu.VMEM((2, CORE_ROWS, 128), BF),
            pltpu.VMEM((16, 2, PIECE, 128), BF),
            pltpu.VMEM((16, 2, PIECE, 128), BF),
            pltpu.VMEM((2, PIECE, 128), BF),
            pltpu.VMEM((3, PIECE, 128), BF),
            pltpu.VMEM((ROWS, 128), BF),
            pltpu.SemaphoreType.DMA((16,)),
            pltpu.SemaphoreType.DMA((38,)),
            pltpu.SemaphoreType.DMA((38,)),
            pltpu.SemaphoreType.DMA((50,)),
            pltpu.SemaphoreType.DMA((50,)),
        ],
        compiler_params=pltpu.CompilerParams(
            collective_id=0, has_side_effects=True, vmem_limit_bytes=44 * 2**20
        ),
    )(*[pltpu.with_memory_space_constraint(a, pltpu.HBM) for a in operands])


def finish_kernel(
    out,
    total,
    output,
    g_first,
    g_first_bias,
    g_mid,
    g_mid_bias,
    g_last,
    g_side,
    g_last_bias,
    out_sem,
):
    writes = [pltpu.make_async_copy(out.at[k], output.at[k], out_sem.at[k]) for k in range(PARTS)]
    for made in writes:
        made.start()

    def rows(at, count):
        return total[at : at + count, :].astype(F32)

    for k in range(2):
        g_first[:, k * 128 : k * 128 + 128] = rows(ROW_FIRST + k * 64, 64)
    for k in range(9):
        g_mid[k // 3, k % 3] = rows(ROW_MID + k * 64, 64)
    bias = rows(ROW_BIAS, 16)
    for k in range(4):
        lanes = slice(k * 128, k * 128 + 128)
        g_last[:, lanes] = rows(ROW_LAST + k * 64, 64)
        g_side[:, lanes] = rows(ROW_SIDE + k * 128, 128)
        g_last_bias[:, lanes] = bias[2 + k : 3 + k, :]
    ch = lax.axis_index("ch")
    g_first_bias[...] = jnp.where(ch == 0, bias[0:1, 0:64], bias[0:1, 64:128])
    g_mid_bias[...] = bias[1:2, 0:64]
    for made in writes:
        made.wait()


def finish(out, total):
    vmem = pl.BlockSpec(memory_space=pltpu.VMEM)
    return pl.pallas_call(
        finish_kernel,
        in_specs=[vmem, vmem],
        out_specs=(pl.BlockSpec(memory_space=pl.ANY), *[vmem] * 7),
        out_shape=(
            jax.ShapeDtypeStruct(out.shape, BF),
            *[
                jax.ShapeDtypeStruct(shape, F32)
                for shape in (
                    (64, 256),
                    (1, 64),
                    (3, 3, 64, 128),
                    (1, 64),
                    (64, 512),
                    (128, 512),
                    (1, 512),
                )
            ],
        ),
        scratch_shapes=[
            pltpu.SemaphoreType.DMA((PARTS,)),
        ],
        compiler_params=pltpu.CompilerParams(vmem_limit_bytes=16 * 2**20),
    )(out, total)


def per_device(
    features,
    cotangent,
    neighbours,
    first_weight,
    first_bias,
    mid_weight,
    mid_bias,
    last_weight,
    side_weight,
    last_bias,
):
    out, total = block(
        features,
        cotangent.reshape(4096, 512),
        neighbours,
        first_weight,
        first_bias.reshape(1, 128),
        mid_weight.transpose(0, 1, 3, 2).reshape(576, 128),
        mid_bias.reshape(1, 128),
        last_weight,
        side_weight,
        last_bias.reshape(1, 512),
    )
    output, g_first, g_first_bias, g_mid, g_mid_bias, g_last, g_side, g_last_bias = finish(
        out.reshape(PARTS, 4096 // PARTS, 512), total
    )
    return (
        output.reshape(4, 32, 32, 512),
        g_first.T,
        g_first_bias.reshape(64),
        g_mid.transpose(0, 1, 3, 2),
        g_mid_bias.reshape(64),
        g_last,
        g_side,
        g_last_bias.reshape(512),
    )


def solution(mesh):
    return jax.shard_map(
        per_device,
        mesh=mesh,
        in_specs=(
            P("tile", None, None, None),
            P("tile", None, None, None),
            P("tile", None),
            P(),
            P(),
            P(None, None, None, "ch"),
            P(),
            P("ch", None),
            P("ch", None),
            P(),
        ),
        out_specs=(
            P("tile", None, None, None),
            P(None, "ch"),
            P("ch"),
            P(None, None, None, "ch"),
            P("ch"),
            P("ch", None),
            P("ch", None),
            P(),
        ),
        check_vma=False,
    )
```

```python
import math

import jax
import jax.numpy as jnp
from jax import lax
from jax.experimental import pallas as pl
from jax.experimental.pallas import tpu as pltpu
from jax.sharding import PartitionSpec as P

BF = jnp.bfloat16
F32 = jnp.float32
MESH = pl.DeviceIdType.MESH

ROW_FIRST = 0
ROW_MID = 128
ROW_LAST = 704
ROW_SIDE = 960
ROW_BIAS = 1472
ROWS = 1536
CORE_ROWS = ROWS // 2
PIECE = CORE_ROWS // 16

CORNERS = ((0, 1, 31), (2, 1, 0), (5, 0, 31), (7, 0, 0))
PLACES = ((0, 0, 7), (2, 0, 40), (5, 33, 7), (7, 33, 40))

CHUNK = 512
FAR_FIRST = (10, 6, 14, 9, 11, 5, 7, 13, 15, 2, 8, 1, 3, 4, 12)
PARTS = 8


def place():
    tile = lax.axis_index("tile")
    ch = lax.axis_index("ch")
    return tile // 16, (tile // 8) % 2, (tile // 2) % 4, tile % 2, ch


def device(y, zh, x, core, ch):
    return (((y * 2 + zh) * 4 + x) * 2 + core, ch)


def sigmoid(v):
    return 0.5 + 0.5 * jnp.tanh(0.5 * v)


def dot(a, b):
    return jnp.dot(a, b, preferred_element_type=F32)


def dot_nt(a, b):
    return lax.dot_general(a, b, (((1,), (1,)), ((), ())), preferred_element_type=F32)


def dot_tn(a, b):
    return lax.dot_general(a, b, (((0,), (0,)), ((), ())), preferred_element_type=F32)


def block_kernel(
    scale,
    features,
    cotangent,
    neighbours,
    w1_h,
    b1_h,
    wm_h,
    mid_bias_h,
    wl_h,
    ws_h,
    last_bias_h,
    out,
    total,
    feat,
    cot,
    near,
    near_s,
    w1,
    b1,
    wm,
    mid_bias_n,
    wl_part,
    ws_part,
    last_bias,
    wide,
    edges,
    table,
    table_out,
    table_s,
    every,
    pack,
    got_first,
    got_second,
    piece,
    halo,
    mid_bias,
    wf,
    wbt,
    wl,
    ws,
    first_slope,
    feat_t,
    rim_slope,
    padded,
    patches,
    mid_delta,
    spread,
    rim,
    g_first,
    g_mid,
    g_last,
    g_side,
    g_first_bias,
    g_mid_bias,
    g_last_bias,
    g_first_t,
    grads,
    from_core,
    by_piece,
    from_plane,
    mine,
    from_z,
    local_sem,
    send_sem,
    recv_sem,
    sum_send_sem,
    sum_recv_sem,
):
    y, zh, x, core, ch = place()
    row_role = core == 0
    along = jnp.where(row_role, x, y)
    across = jnp.where(row_role, y, x)
    own_place = y * 4 + x

    def gather_peer(step):
        to = lax.rem(along + step, 4)
        return device(jnp.where(row_role, y, to), zh, jnp.where(row_role, to, x), core, ch)

    def select_peer(step):
        to = lax.rem(across + step, 4)
        return device(jnp.where(row_role, to, y), zh, jnp.where(row_role, x, to), core, ch)

    def plane_place(step, back=False):
        rows, columns = step // 4, step % 4
        if back:
            rows, columns = 4 - rows, 4 - columns
        return lax.rem(y + rows, 4) * 4 + lax.rem(x + columns, 4)

    def plane_peer(step):
        to = plane_place(step)
        return device(to // 4, zh, to % 4, core, ch)

    sibling = device(y, zh, x, 1 - core, ch)
    z_peers = [device(y, 1 - zh, x, role, 1 - ch) for role in (0, 1)]
    ch_same = device(y, zh, x, core, 1 - ch)
    ch_cross = device(y, zh, x, 1 - core, 1 - ch)
    z_even = device(y, 1 - zh, x, core, ch)
    z_odd = device(y, 1 - zh, x, core, 1 - ch)

    barrier = pltpu.get_barrier_semaphore()
    greeted = [sibling, *z_peers, ch_same, ch_cross, z_even]
    greeted += [plane_peer(step) for step in range(1, 16)]
    for peer in greeted:
        pl.semaphore_signal(barrier, inc=1, device_id=peer, device_id_type=MESH)

    loads = [
        (neighbours, near),
        (neighbours, near_s),
        *[(features.at[tile], feat.at[tile]) for tile in range(4)],
        (w1_h, w1),
        (b1_h, b1),
        (wm_h, wm.at[0]),
        (wl_h, wl_part.at[0]),
        (ws_h, ws_part.at[0]),
        (mid_bias_h, mid_bias_n),
        (last_bias_h, last_bias),
    ]
    loads += [
        (cotangent.at[pl.ds(pl.multiple_of((2 * ch + k) * 1024, 1024), 1024)], cot.at[k])
        for k in range(2)
    ]
    loading = []
    for number, (source, target) in enumerate(loads):
        made = pltpu.make_async_copy(source, target, local_sem.at[number])
        made.start()
        loading.append(made)

    loading[0].wait()
    ids = jnp.minimum(near[...], 255)
    in_y, in_zh, in_x, low = ids >> 6, (ids >> 5) & 1, (ids >> 3) & 3, ids & 7
    by_row = in_zh * 32 + in_x * 8 + low + 64 * in_y
    by_col = in_zh * 32 + in_y * 8 + low + 64 * in_x
    role = jnp.zeros_like(ids) + core
    table[across, core] = jnp.zeros((8, 128), jnp.int32)
    table[across, core, 0:4, 0:8] = jnp.where(role == 0, by_row, by_col)
    table_out[...] = jnp.zeros((8, 128), jnp.int32)
    table_out[0:4, 0:8] = jnp.where(role == 0, by_col, by_row)

    for tile in range(4):
        loading[2 + tile].wait()
        first_row = feat[tile, 0]
        last_row = feat[tile, 31]
        for half in range(2):
            lanes = slice(half * 128, half * 128 + 128)
            wide[0:512, :] = feat[tile, :, 0:16, lanes].astype(F32).reshape(512, 128)
            wide[512:1024, :] = feat[tile, :, 16:32, lanes].astype(F32).reshape(512, 128)
            edges[0, half, tile, 0] = first_row[:, lanes]
            edges[0, half, tile, 1] = last_row[:, lanes]
            edges[1, half, tile, 0] = wide[pl.ds(0, 32, stride=16), :].astype(BF)
            edges[1, half, tile, 1] = wide[pl.ds(527, 32, stride=16), :].astype(BF)

    def part(plane, at, owner):
        return pl.ds(pl.multiple_of(plane * 32 + at * 8 + owner * 4, 4), 4)

    every[part(zh, along, core)] = edges[core, ch]
    for number in (8, 9, 10):
        loading[number].wait()

    pl.semaphore_wait(barrier, len(greeted))

    sent = []

    def copy(number, source, target, peer, arrives):
        return pltpu.make_async_remote_copy(
            src_ref=source,
            dst_ref=target,
            send_sem=send_sem.at[number],
            recv_sem=recv_sem.at[arrives],
            device_id=peer,
            device_id_type=MESH,
        )

    def start(number, source, target, peer, arrives):
        made = copy(number, source, target, peer, arrives)
        made.start()
        sent.append(made)

    def arrived(number, target):
        copy(0, target, target, sibling, number).wait_recv()

    def first_layer(turn):
        tile = lax.rem(2 * ch + turn, 4)
        pixels = feat[tile].reshape(1024, 256)
        pre = dot(pixels, w1[...]) + b1[...]
        sig = sigmoid(pre)
        act = pre * sig
        padded[tile, 1:33, 8:40, :] = act.reshape(32, 32, 128)
        if turn < 2:
            first_slope[turn] = sig + act * (1.0 - sig)
            feat_t[turn] = pixels.T

    start(1, edges.at[1 - core, ch], every.at[part(zh, across, core)], sibling, 1)
    for k in range(2):
        start(
            2 + k,
            edges.at[k, 1 - ch],
            every.at[part(zh, x if k == 0 else y, core)],
            z_peers[k],
            2 + core,
        )
    def ring(far, owner):
        strips = every.at[part(1 - zh if far else zh, along, owner)]
        first = 30 + (far * 2 + owner) * 3
        for k in range(3):
            start(first + k, strips, strips, gather_peer(k + 1), first + k)

    ring(0, core)
    start(0, table_out, table.at[along, core], sibling, 0)
    start(4, wm.at[0], wm.at[1], ch_same, 4)
    start(5, wl_part.at[0], wl_part.at[1], ch_same, 5)
    start(6, ws_part.at[0], ws_part.at[1], ch_same, 6)
    loading[6].wait()
    loading[7].wait()
    first_layer(0)

    arrived(1, every.at[part(zh, along, 1 - core)])
    ring(0, 1 - core)
    arrived(0, table.at[across, 1 - core])
    for step in range(1, 4):
        start(8 + step, table.at[across], table.at[across], select_peer(step), 8 + step)
    for owner in range(2):
        arrived(2 + owner, every.at[part(1 - zh, along, owner)])
        ring(1, owner)
    first_layer(1)
    before = lax.rem(along + 3, 4)
    after = lax.rem(along + 1, 4)
    opposite = lax.rem(along + 2, 4)
    for step in range(1, 4):
        arrived(8 + step, table.at[lax.rem(across + 4 - step, 4)])
    to_scalars = pltpu.make_async_copy(table, table_s, local_sem.at[len(loads)])
    to_scalars.start()
    first_layer(2)
    arrived(4, wm.at[1])
    arrived(5, wl_part.at[1])
    arrived(6, ws_part.at[1])
    for number in (11, 12):
        loading[number].wait()
    for i in range(3):
        for half in range(2):
            at = i * 128 + half * 64
            for j in range(3):
                source = (i * 3 + j) * 64
                wbt[at : at + 64, j * 128 : j * 128 + 128] = wm[half, source : source + 64, :]
        wf[i] = wbt[i * 128 : i * 128 + 128, :].astype(F32).T.astype(BF)
    own128 = pl.multiple_of(ch * 128, 128)
    other128 = pl.multiple_of((1 - ch) * 128, 128)
    wl[0:64, :] = wl_part[0]
    wl[64:128, :] = wl_part[1]
    ws[pl.ds(own128, 128), :] = ws_part[0]
    ws[pl.ds(other128, 128), :] = ws_part[1]
    bias = mid_bias_n[...]
    swapped = jnp.concatenate([bias[:, 64:128], bias[:, 0:64]], axis=1)
    mid_bias[...] = jnp.where(ch == 0, bias, swapped)
    for ref in (g_first, g_mid, g_last, g_side, g_first_bias, g_mid_bias, g_last_bias):
        ref[...] = jnp.zeros_like(ref)
    blank = jnp.zeros((32, 128), BF)
    for line, lanes in ((32, 0), (33, 0), (0, 128), (33, 128), (0, 256), (1, 256)):
        mid_delta[line, :, lanes : lanes + 128] = blank
    to_scalars.wait()
    for far, plane in enumerate((zh, 1 - zh)):
        for owner in range(2):
            first = 30 + (far * 2 + owner) * 3
            for k, origin in enumerate((before, opposite, after)):
                arrived(first + k, every.at[part(plane, origin, owner)])

    first_dir = 1 + 2 * core
    second_dir = 6 - 2 * core
    rows16 = lax.broadcasted_iota(jnp.int32, (16, 128), 0)

    got = (got_first, got_second)

    def pack_round(step, turn):
        wanted = lax.rem(across + step, 4)
        into = pack.at[step, turn] if step else got[turn].at[0]

        def pack_tile(slot, corners):
            owner, tile = slot // 2, turn + 2 * (slot % 2)

            def held(d):
                return table_s[wanted, owner, tile, d] & 63

            at = slot * 64
            into[pl.ds(at, 32), :] = every[held(first_dir), 1]
            into[pl.ds(at + 32, 32), :] = every[held(second_dir), 0]
            for k, (d, which, line) in enumerate(CORNERS):
                rows = every[held(d), which, 16 * (line // 16) : 16 * (line // 16) + 16, :]
                row = rows.astype(F32)[line % 16 : line % 16 + 1]
                corners = jnp.where(rows16 == slot * 4 + k, row, corners)
            return corners

        corners = jnp.zeros((16, 128), F32)
        for slot in range(4):
            corners = pack_tile(slot, corners)
        into[256:272, :] = corners.astype(BF)
        if step:
            number = 17 + turn * 3 + step
            start(number, pack.at[step, turn], got[turn].at[step], select_peer(step), number)

    def finish_round(owner, turn):
        def finish_tile(k, corners):
            slot, tile = owner * 2 + k, turn + 2 * k

            def chosen(d, rows):
                from_step = (across + 4 - (table_s[across, owner, tile, d] >> 6)) & 3
                return got[turn][from_step, rows, :]

            at = pl.multiple_of(slot * 64, 64)
            to = k * 64
            piece[turn, owner, pl.ds(to, 32), :] = chosen(first_dir, pl.ds(at, 32))
            piece[turn, owner, pl.ds(to + 32, 32), :] = chosen(second_dir, pl.ds(at + 32, 32))
            for c, (d, _, _) in enumerate(CORNERS):
                rows = chosen(d, slice(256, 272)).astype(F32)
                corners = jnp.where(rows16 == slot * 4 + c, rows, corners)
            return corners

        corners = jnp.zeros((16, 128), F32)
        for k in range(2):
            corners = finish_tile(k, corners)
        half = jnp.where(owner == 0, corners[0:8], corners[8:16])
        both = jnp.concatenate([half, half], axis=0)
        piece[turn, owner, 128:144, :] = both.astype(BF)

    for turn in range(2):
        for step in (2, 1, 3):
            pack_round(step, turn)
    pack_round(0, 0)
    pack_round(0, 1)
    first_layer(3)
    for turn in range(2):
        for step in range(1, 4):
            arrived(17 + turn * 3 + step, got[turn].at[step])
        for owner, copies in (
            (1 - core, ((0, ch_cross), (1, sibling))),
            (core, ((2, ch_same),)),
        ):
            finish_round(owner, turn)
            for k, peer in copies:
                number = 24 + turn * 3 + k
                start(number, piece.at[turn, owner], halo.at[core, ch, turn], peer, number)
        halo[core, ch, turn] = piece[turn, core]

    def halo_arrived(turn):
        arrived(24 + turn * 3, halo.at[1 - core, 1 - ch, turn])
        arrived(25 + turn * 3, halo.at[1 - core, ch, turn])
        arrived(26 + turn * 3, halo.at[core, 1 - ch, turn])

    loading[1].wait()


    def here(tile, direction):
        return jnp.where(near_s[tile, direction] < 256, 1.0, 0.0).astype(F32)

    def rim_features(turn, which):
        rows = pl.ds(pl.multiple_of(which * 64, 64), 64)
        parts = [(0, rows), (1, rows), (0, slice(128, 144))]
        return jnp.concatenate(
            [jnp.concatenate([halo[r, h, turn, at, :] for h in range(2)], axis=1) for r, at in parts],
            axis=0,
        )

    def pad(tile, turn, which):
        pre = dot(rim_features(turn, which), w1[...]) + b1[...]
        sig = sigmoid(pre)
        act = pre * sig
        rim_slope[...] = sig + act * (1.0 - sig)
        rim[...] = act
        padded[tile, 0, 8:40, :] = act[0:32] * here(tile, 1)
        padded[tile, 33, 8:40, :] = act[32:64] * here(tile, 6)
        padded[tile, 1:33, 7:8, :] = (act[64:96] * here(tile, 3)).reshape(32, 1, 128)
        padded[tile, 1:33, 40:41, :] = (act[96:128] * here(tile, 4)).reshape(32, 1, 128)
        for k, (d, line, column) in enumerate(PLACES):
            row = rim[pl.ds(128 + which * 4 + k, 1), :]
            padded[tile, line, column : column + 1, :] = row * here(tile, d)
        for j in range(3):
            patches[:, :, j * 128 : j * 128 + 128] = padded[tile, :, 7 + j : 39 + j, :].astype(BF)

    high = CHUNK // 32

    def forward(tile, number):
        row = pl.multiple_of(number * CHUNK, CHUNK)
        line = number * high
        views = [patches[pl.ds(line + i, high)].reshape(CHUNK, 384) for i in range(3)]
        mid_pre = mid_bias[...] + dot(views[0], wf[0]) + dot(views[1], wf[1]) + dot(views[2], wf[2])
        mid_sig = sigmoid(mid_pre)
        mid_val = mid_pre * mid_sig
        mid_act = mid_val.astype(BF)
        x_part = feat[tile, pl.ds(line, high)].reshape(CHUNK, 256)
        out_pre = dot(mid_act, wl[...]) + dot(x_part, ws[...]) + last_bias[...]
        sig = sigmoid(out_pre)
        val = out_pre * sig
        out[tile, pl.ds(row, CHUNK), :] = val.astype(BF)
        return row, line, views, mid_sig, mid_val, mid_act, x_part, sig, val

    def forward_tile(tile, first, last):
        def body(number, carry):
            forward(tile, number)
            return carry

        lax.fori_loop(first, last, body, 0, unroll=True)

    def whole_tile(k, carry):
        tile = 2 * ch + k
        halo_arrived(k)
        pad(tile, k, ch)

        def body(number, inner):
            row, line, views, mid_sig, mid_val, mid_act, x_part, sig, val = forward(tile, number)
            slope = sig + val * (1.0 - sig)
            grad_out = (cot[k, pl.ds(row, CHUNK), :].astype(F32) * scale * slope).astype(BF)
            g_last[...] += dot_tn(mid_act, grad_out)
            g_side[...] += dot(feat_t[k, :, pl.ds(row, CHUNK)], grad_out)
            g_last_bias[...] += grad_out.astype(F32).reshape(CHUNK // 8, 8, 512).sum(axis=0)
            mid_back = dot_nt(grad_out, wl[...])
            delta = (mid_back * (mid_sig + mid_val * (1.0 - mid_sig))).astype(BF)
            g_mid_bias[...] += delta.astype(F32).reshape(CHUNK // 8, 8, 128).sum(axis=0)
            for i in range(3):
                g_mid[i] += dot_tn(delta, views[i])
            for i in range(3):
                mid_delta[pl.ds(line + i, high), :, i * 128 : i * 128 + 128] = delta.reshape(
                    high, 32, 128
                )
            return inner

        lax.fori_loop(0, 1024 // CHUNK, body, 0, unroll=True)

        back = dot(mid_delta[...].reshape(1088, 384), wbt[...]).reshape(34, 32, 384)
        spread[:, 0:8, :] = jnp.zeros((34, 8, 128), F32)
        spread[:, 40:48, :] = jnp.zeros((34, 8, 128), F32)
        spread[:, 8:40, :] = back[:, :, 128:256]
        spread[:, 7:39, :] += back[:, :, 0:128]
        spread[:, 9:41, :] += back[:, :, 256:384]

        delta = (spread[1:33, 8:40, :].reshape(1024, 128) * first_slope[k]).astype(BF)
        rim[...] = jnp.zeros_like(rim)
        rim[0:32, :] = spread[0, 8:40, :] * here(tile, 1)
        rim[32:64, :] = spread[33, 8:40, :] * here(tile, 6)
        rim[64:96, :] = spread[1:33, 7:8, :].reshape(32, 128) * here(tile, 3)
        rim[96:128, :] = spread[1:33, 40:41, :].reshape(32, 128) * here(tile, 4)
        for c, (d, line, column) in enumerate(PLACES):
            row = spread[line, column : column + 1, :]
            rim[pl.ds(128 + ch * 4 + c, 1), :] = row * here(tile, d)
        delta_rim = (rim[...] * rim_slope[...]).astype(BF)
        g_first[...] += dot(feat_t[k], delta) + dot_tn(rim_features(k, ch), delta_rim)
        g_first_bias[...] += delta.astype(F32).reshape(128, 8, 128).sum(axis=0)
        g_first_bias[...] += delta_rim.astype(F32).reshape(18, 8, 128).sum(axis=0)
        return carry

    loading[13].wait()
    loading[14].wait()
    lax.fori_loop(0, 2, whole_tile, 0)


    g_first_t[...] = g_first[...].T
    bias_first = jnp.sum(g_first_bias[...], axis=0, keepdims=True)
    bias_mid = jnp.sum(g_mid_bias[...], axis=0, keepdims=True)
    bias_last = jnp.sum(g_last_bias[...], axis=0, keepdims=True)
    for half in range(2):
        whose = ch if half == 0 else 1 - ch
        start64 = pl.multiple_of(whose * 64, 64)
        start128 = pl.multiple_of(whose * 128, 128)
        order = slice(half * 64, half * 64 + 64)
        for k in range(2):
            at = ROW_FIRST + k * 64
            lanes = slice(k * 128, k * 128 + 128)
            grads[half, at : at + 64, :] = g_first_t[pl.ds(start64, 64), lanes].astype(BF)
        for i in range(3):
            for j in range(3):
                at = ROW_MID + (i * 3 + j) * 64
                lanes = slice(j * 128, j * 128 + 128)
                grads[half, at : at + 64, :] = g_mid[i, order, lanes].astype(BF)
        for k in range(4):
            lanes = slice(k * 128, k * 128 + 128)
            at = ROW_LAST + k * 64
            grads[half, at : at + 64, :] = g_last[order, lanes].astype(BF)
            at = ROW_SIDE + k * 128
            grads[half, at : at + 128, :] = g_side[pl.ds(start128, 128), lanes].astype(BF)
        mid_row = bias_mid
        if half == 1:
            mid_row = jnp.concatenate([bias_mid[:, 64:128], bias_mid[:, 0:64]], axis=1)
        rows = jnp.where(rows16 == 0, bias_first, jnp.where(rows16 == 1, mid_row, 0.0))
        for k in range(4):
            rows = jnp.where(rows16 == 2 + k, bias_last[:, k * 128 : k * 128 + 128], rows)
        grads[half, ROW_BIAS : ROW_BIAS + 16, :] = rows.astype(BF)
        grads[half, ROW_BIAS + 16 : ROWS, :] = jnp.zeros((ROWS - ROW_BIAS - 16, 128), BF)


    def hand(number, source, target, peer):
        made = pltpu.make_async_remote_copy(
            src_ref=source,
            dst_ref=target,
            send_sem=sum_send_sem.at[number],
            recv_sem=sum_recv_sem.at[number],
            device_id=peer,
            device_id_type=MESH,
        )
        made.start()
        sent.append(made)
        return made

    third = lax.rem(2 + 2 * ch, 4)
    fourth = lax.rem(3 + 2 * ch, 4)
    count = 1024 // CHUNK

    own_rows = pl.multiple_of(core * CORE_ROWS, CORE_ROWS)
    other_rows = pl.multiple_of((1 - core) * CORE_ROWS, CORE_ROWS)
    swap = hand(0, grads.at[:, pl.ds(other_rows, CORE_ROWS)], from_core, sibling)
    pad(third, 0, 1 - ch)
    swap.wait_recv()
    for half in range(2):
        added = grads[half, pl.ds(own_rows, CORE_ROWS), :].astype(F32) + from_core[half].astype(F32)
        by_piece[:, half] = added.astype(BF).reshape(16, PIECE, 128)
    plane = []
    for step in FAR_FIRST:
        piece_of = by_piece.at[plane_place(step)]
        plane.append((step, hand(step, piece_of, from_plane.at[step], plane_peer(step))))
    forward_tile(third, 0, count)
    added = by_piece[own_place].astype(F32)
    for step, made in reversed(plane):
        made.wait_recv()
        added = added + from_plane[step].astype(F32)
    mine[...] = added.astype(BF)
    hops = []
    for k, (half, peer) in enumerate(((0, z_even), (1, ch_same), (1, z_odd))):
        hops.append(hand(16 + k, mine.at[half], from_z.at[k], peer))
    pad(fourth, 1, 1 - ch)
    forward_tile(fourth, 0, count // 2)
    added = added[0]
    for k, made in enumerate(hops):
        made.wait_recv()
        added = added + from_z[k].astype(F32)
    at = pl.multiple_of(own_rows + own_place * PIECE, 16)
    total[pl.ds(at, PIECE), :] = added.astype(BF)
    def cross(step):
        origin = plane_place(step, back=True)
        rows = total.at[pl.ds(pl.multiple_of(own_rows + origin * PIECE, 16), PIECE)]
        return hand(34 + step, rows, rows, sibling)

    backs, crossings = [], []
    for step in FAR_FIRST:
        here_too = total.at[pl.ds(at, PIECE)]
        backs.append((step, hand(18 + step, here_too, here_too, plane_peer(step))))
    crossings.append(cross(0))
    forward_tile(fourth, count // 2, count)
    for step, made in reversed(backs):
        made.wait_recv()
        crossings.append(cross(step))
    for made in crossings:
        made.wait_recv()
    for made in sent:
        made.wait_send()


def block(*operands):
    scale = 1.0 / math.sqrt(4096)
    anywhere = pl.BlockSpec(memory_space=pl.ANY)

    def kernel(*refs):
        block_kernel(scale, *refs)

    return pl.pallas_call(
        kernel,
        in_specs=[anywhere] * 10,
        out_specs=(pl.BlockSpec(memory_space=pltpu.VMEM),) * 2,
        out_shape=(
            jax.ShapeDtypeStruct((4, 1024, 512), BF),
            jax.ShapeDtypeStruct((ROWS, 128), BF),
        ),
        scratch_shapes=[
            pltpu.VMEM((4, 32, 32, 256), BF),
            pltpu.VMEM((2, 1024, 512), BF),
            pltpu.VMEM((4, 8), jnp.int32),
            pltpu.SMEM((4, 8), jnp.int32),
            pltpu.VMEM((256, 128), BF),
            pltpu.VMEM((1, 128), F32),
            pltpu.VMEM((2, 576, 128), BF),
            pltpu.VMEM((1, 128), F32),
            pltpu.VMEM((2, 64, 512), BF),
            pltpu.VMEM((2, 128, 512), BF),
            pltpu.VMEM((1, 512), F32),
            pltpu.VMEM((1024, 128), F32),
            pltpu.VMEM((2, 2, 4, 2, 32, 128), BF),
            pltpu.VMEM((4, 2, 8, 128), jnp.int32),
            pltpu.VMEM((8, 128), jnp.int32),
            pltpu.SMEM((4, 2, 8, 128), jnp.int32),
            pltpu.VMEM((64, 2, 32, 128), BF),
            pltpu.VMEM((4, 2, 272, 128), BF),
            pltpu.VMEM((4, 272, 128), BF),
            pltpu.VMEM((4, 272, 128), BF),
            pltpu.VMEM((2, 2, 144, 128), BF),
            pltpu.VMEM((2, 2, 2, 144, 128), BF),
            pltpu.VMEM((1, 128), F32),
            pltpu.VMEM((3, 384, 128), BF),
            pltpu.VMEM((384, 384), BF),
            pltpu.VMEM((128, 512), BF),
            pltpu.VMEM((256, 512), BF),
            pltpu.VMEM((2, 1024, 128), F32),
            pltpu.VMEM((2, 256, 1024), BF),
            pltpu.VMEM((144, 128), F32),
            pltpu.VMEM((4, 34, 48, 128), F32),
            pltpu.VMEM((34, 32, 384), BF),
            pltpu.VMEM((34, 32, 384), BF),
            pltpu.VMEM((34, 48, 128), F32),
            pltpu.VMEM((144, 128), F32),
            pltpu.VMEM((256, 128), F32),
            pltpu.VMEM((3, 128, 384), F32),
            pltpu.VMEM((128, 512), F32),
            pltpu.VMEM((256, 512), F32),
            pltpu.VMEM((8, 128), F32),
            pltpu.VMEM((8, 128), F32),
            pltpu.VMEM((8, 512), F32),
            pltpu.VMEM((128, 256), F32),
            pltpu.VMEM((2, ROWS, 128), BF),
            pltpu.VMEM((2, CORE_ROWS, 128), BF),
            pltpu.VMEM((16, 2, PIECE, 128), BF),
            pltpu.VMEM((16, 2, PIECE, 128), BF),
            pltpu.VMEM((2, PIECE, 128), BF),
            pltpu.VMEM((3, PIECE, 128), BF),
            pltpu.SemaphoreType.DMA((16,)),
            pltpu.SemaphoreType.DMA((42,)),
            pltpu.SemaphoreType.DMA((42,)),
            pltpu.SemaphoreType.DMA((50,)),
            pltpu.SemaphoreType.DMA((50,)),
        ],
        compiler_params=pltpu.CompilerParams(
            collective_id=0, has_side_effects=True, vmem_limit_bytes=44 * 2**20
        ),
    )(*[pltpu.with_memory_space_constraint(a, pltpu.HBM) for a in operands])


def finish_kernel(
    out,
    total,
    output,
    g_first,
    g_first_bias,
    g_mid,
    g_mid_bias,
    g_last,
    g_side,
    g_last_bias,
    first_v,
    mid_v,
    last_v,
    side_v,
    out_sem,
):
    writes = [pltpu.make_async_copy(out.at[k], output.at[k], out_sem.at[k]) for k in range(PARTS)]
    for made in writes:
        made.start()

    def send(number, source, target):
        made = pltpu.make_async_copy(source, target, out_sem.at[PARTS + number])
        made.start()
        writes.append(made)

    def rows(at, count):
        return total[at : at + count, :].astype(F32)

    for k in range(4):
        lanes = slice(k * 128, k * 128 + 128)
        side_v[:, lanes] = rows(ROW_SIDE + k * 128, 128)
        last_v[:, lanes] = rows(ROW_LAST + k * 64, 64)
    send(0, side_v, g_side)
    send(1, last_v, g_last)
    for k in range(9):
        mid_v[k // 3, k % 3] = rows(ROW_MID + k * 64, 64)
    send(2, mid_v, g_mid)
    for k in range(2):
        first_v[:, k * 128 : k * 128 + 128] = rows(ROW_FIRST + k * 64, 64)
    send(3, first_v, g_first)
    bias = rows(ROW_BIAS, 16)
    for k in range(4):
        lanes = slice(k * 128, k * 128 + 128)
        g_last_bias[:, lanes] = bias[2 + k : 3 + k, :]
    ch = lax.axis_index("ch")
    g_first_bias[...] = jnp.where(ch == 0, bias[0:1, 0:64], bias[0:1, 64:128])
    g_mid_bias[...] = bias[1:2, 0:64]
    for made in writes:
        made.wait()


def finish(out, total):
    vmem = pl.BlockSpec(memory_space=pltpu.VMEM)
    anywhere = pl.BlockSpec(memory_space=pl.ANY)
    return pl.pallas_call(
        finish_kernel,
        in_specs=[vmem, vmem],
        out_specs=(anywhere, anywhere, vmem, anywhere, vmem, anywhere, anywhere, vmem),
        out_shape=(
            jax.ShapeDtypeStruct(out.shape, BF),
            *[
                jax.ShapeDtypeStruct(shape, F32)
                for shape in (
                    (64, 256),
                    (1, 64),
                    (3, 3, 64, 128),
                    (1, 64),
                    (64, 512),
                    (128, 512),
                    (1, 512),
                )
            ],
        ),
        scratch_shapes=[
            pltpu.VMEM((64, 256), F32),
            pltpu.VMEM((3, 3, 64, 128), F32),
            pltpu.VMEM((64, 512), F32),
            pltpu.VMEM((128, 512), F32),
            pltpu.SemaphoreType.DMA((PARTS + 4,)),
        ],
        compiler_params=pltpu.CompilerParams(vmem_limit_bytes=16 * 2**20),
    )(out, total)


def per_device(
    features,
    cotangent,
    neighbours,
    first_weight,
    first_bias,
    mid_weight,
    mid_bias,
    last_weight,
    side_weight,
    last_bias,
):
    out, total = block(
        features,
        cotangent.reshape(4096, 512),
        neighbours,
        first_weight,
        first_bias.reshape(1, 128),
        mid_weight.transpose(0, 1, 3, 2).reshape(576, 128),
        mid_bias.reshape(1, 128),
        last_weight,
        side_weight,
        last_bias.reshape(1, 512),
    )
    output, g_first, g_first_bias, g_mid, g_mid_bias, g_last, g_side, g_last_bias = finish(
        out.reshape(PARTS, 4096 // PARTS, 512), total
    )
    return (
        output.reshape(4, 32, 32, 512),
        g_first.T,
        g_first_bias.reshape(64),
        g_mid.transpose(0, 1, 3, 2),
        g_mid_bias.reshape(64),
        g_last,
        g_side,
        g_last_bias.reshape(512),
    )


def solution(mesh):
    return jax.shard_map(
        per_device,
        mesh=mesh,
        in_specs=(
            P("tile", None, None, None),
            P("tile", None, None, None),
            P("tile", None),
            P(),
            P(),
            P(None, None, None, "ch"),
            P(),
            P("ch", None),
            P("ch", None),
            P(),
        ),
        out_specs=(
            P("tile", None, None, None),
            P(None, "ch"),
            P("ch"),
            P(None, None, None, "ch"),
            P("ch"),
            P("ch", None),
            P("ch", None),
            P(),
        ),
        check_vma=False,
    )
```

```python
import math

import jax
import jax.numpy as jnp
from jax import lax
from jax.experimental import pallas as pl
from jax.experimental.pallas import tpu as pltpu
from jax.sharding import PartitionSpec as P

BF = jnp.bfloat16
F32 = jnp.float32
MESH = pl.DeviceIdType.MESH

ROW_FIRST = 0
ROW_MID = 128
ROW_LAST = 704
ROW_SIDE = 960
ROW_BIAS = 1472
ROWS = 1536
CORE_ROWS = ROWS // 2
PIECE = CORE_ROWS // 16

CORNERS = ((0, 1, 31), (2, 1, 0), (5, 0, 31), (7, 0, 0))
PLACES = ((0, 0, 7), (2, 0, 40), (5, 33, 7), (7, 33, 40))

CHUNK = 512
FAR_FIRST = (10, 6, 14, 9, 11, 5, 7, 13, 15, 2, 8, 1, 3, 4, 12)
PARTS = 8


def place():
    tile = lax.axis_index("tile")
    ch = lax.axis_index("ch")
    return tile // 16, (tile // 8) % 2, (tile // 2) % 4, tile % 2, ch


def device(y, zh, x, core, ch):
    return (((y * 2 + zh) * 4 + x) * 2 + core, ch)


def sigmoid(v):
    return 0.5 + 0.5 * jnp.tanh(0.5 * v)


def dot(a, b):
    return jnp.dot(a, b, preferred_element_type=F32)


def dot_nt(a, b):
    return lax.dot_general(a, b, (((1,), (1,)), ((), ())), preferred_element_type=F32)


def dot_tn(a, b):
    return lax.dot_general(a, b, (((0,), (0,)), ((), ())), preferred_element_type=F32)


def block_kernel(
    scale,
    features,
    cotangent,
    neighbours,
    w1_h,
    b1_h,
    wm_h,
    mid_bias_h,
    wl_h,
    ws_h,
    last_bias_h,
    out,
    total,
    feat,
    cot,
    near,
    near_s,
    w1,
    b1,
    wm,
    mid_bias_n,
    wl_part,
    ws_part,
    last_bias,
    wide,
    edges,
    table,
    table_out,
    table_s,
    every,
    pack,
    got_first,
    got_second,
    piece,
    halo,
    mid_bias,
    wf,
    wbt,
    wl,
    ws,
    first_slope,
    feat_t,
    rim_slope,
    padded,
    patches,
    mid_delta,
    spread,
    rim,
    g_first,
    g_mid,
    g_last,
    g_side,
    g_first_bias,
    g_mid_bias,
    g_last_bias,
    g_first_t,
    grads,
    from_core,
    by_piece,
    from_plane,
    mine,
    from_z,
    local_sem,
    send_sem,
    recv_sem,
    sum_send_sem,
    sum_recv_sem,
):
    y, zh, x, core, ch = place()
    row_role = core == 0
    along = jnp.where(row_role, x, y)
    across = jnp.where(row_role, y, x)
    own_place = y * 4 + x

    def gather_peer(step):
        to = lax.rem(along + step, 4)
        return device(jnp.where(row_role, y, to), zh, jnp.where(row_role, to, x), core, ch)

    def select_peer(step):
        to = lax.rem(across + step, 4)
        return device(jnp.where(row_role, to, y), zh, jnp.where(row_role, x, to), core, ch)

    def plane_place(step, back=False):
        rows, columns = step // 4, step % 4
        if back:
            rows, columns = 4 - rows, 4 - columns
        return lax.rem(y + rows, 4) * 4 + lax.rem(x + columns, 4)

    def plane_peer(step):
        to = plane_place(step)
        return device(to // 4, zh, to % 4, core, ch)

    sibling = device(y, zh, x, 1 - core, ch)
    z_peers = [device(y, 1 - zh, x, role, 1 - ch) for role in (0, 1)]
    ch_same = device(y, zh, x, core, 1 - ch)
    ch_cross = device(y, zh, x, 1 - core, 1 - ch)
    z_even = device(y, 1 - zh, x, core, ch)
    z_odd = device(y, 1 - zh, x, core, 1 - ch)

    barrier = pltpu.get_barrier_semaphore()
    greeted = [sibling, *z_peers, ch_same, ch_cross, z_even]
    greeted += [plane_peer(step) for step in range(1, 16)]
    for peer in greeted:
        pl.semaphore_signal(barrier, inc=1, device_id=peer, device_id_type=MESH)

    loads = [
        (neighbours, near),
        (neighbours, near_s),
        *[(features.at[tile], feat.at[tile]) for tile in range(4)],
        (w1_h, w1),
        (b1_h, b1),
        (wm_h, wm.at[0]),
        (wl_h, wl_part.at[0]),
        (ws_h, ws_part.at[0]),
        (mid_bias_h, mid_bias_n),
        (last_bias_h, last_bias),
    ]
    loads += [
        (cotangent.at[pl.ds(pl.multiple_of((2 * ch + k) * 1024, 1024), 1024)], cot.at[k])
        for k in range(2)
    ]
    loading = []
    for number, (source, target) in enumerate(loads):
        made = pltpu.make_async_copy(source, target, local_sem.at[number])
        if number < 13:
            made.start()
        loading.append(made)

    loading[0].wait()
    ids = jnp.minimum(near[...], 255)
    in_y, in_zh, in_x, low = ids >> 6, (ids >> 5) & 1, (ids >> 3) & 3, ids & 7
    by_row = in_zh * 32 + in_x * 8 + low + 64 * in_y
    by_col = in_zh * 32 + in_y * 8 + low + 64 * in_x
    role = jnp.zeros_like(ids) + core
    table[across, core] = jnp.zeros((8, 128), jnp.int32)
    table[across, core, 0:4, 0:8] = jnp.where(role == 0, by_row, by_col)
    table_out[...] = jnp.zeros((8, 128), jnp.int32)
    table_out[0:4, 0:8] = jnp.where(role == 0, by_col, by_row)

    for tile in range(4):
        loading[2 + tile].wait()
        first_row = feat[tile, 0]
        last_row = feat[tile, 31]
        for half in range(2):
            lanes = slice(half * 128, half * 128 + 128)
            low_columns = feat[tile, :, 0:16, lanes].astype(F32)[:, 0:8]
            high_columns = feat[tile, :, 16:32, lanes].astype(F32)[:, 8:16]
            wide[0:256, :] = low_columns.reshape(256, 128)
            wide[256:512, :] = high_columns.reshape(256, 128)
            edges[0, half, tile, 0] = first_row[:, lanes]
            edges[0, half, tile, 1] = last_row[:, lanes]
            edges[1, half, tile, 0] = wide[pl.ds(0, 32, stride=8), :].astype(BF)
            edges[1, half, tile, 1] = wide[pl.ds(263, 32, stride=8), :].astype(BF)

    def part(plane, at, owner):
        return pl.ds(pl.multiple_of(plane * 32 + at * 8 + owner * 4, 4), 4)

    every[part(zh, along, core)] = edges[core, ch]
    for number in (8, 9, 10):
        loading[number].wait()

    pl.semaphore_wait(barrier, len(greeted))

    sent = []

    def copy(number, source, target, peer, arrives):
        return pltpu.make_async_remote_copy(
            src_ref=source,
            dst_ref=target,
            send_sem=send_sem.at[number],
            recv_sem=recv_sem.at[arrives],
            device_id=peer,
            device_id_type=MESH,
        )

    def start(number, source, target, peer, arrives):
        made = copy(number, source, target, peer, arrives)
        made.start()
        sent.append(made)

    def arrived(number, target):
        copy(0, target, target, sibling, number).wait_recv()

    def first_layer(turn):
        tile = lax.rem(2 * ch + turn, 4)
        pixels = feat[tile].reshape(1024, 256)
        pre = dot(pixels, w1[...]) + b1[...]
        sig = sigmoid(pre)
        act = pre * sig
        padded[tile, 1:33, 8:40, :] = act.reshape(32, 32, 128)
        if turn < 2:
            first_slope[turn] = sig + act * (1.0 - sig)
            feat_t[turn] = pixels.T

    start(1, edges.at[1 - core, ch], every.at[part(zh, across, core)], sibling, 1)
    for k in range(2):
        start(
            2 + k,
            edges.at[k, 1 - ch],
            every.at[part(zh, x if k == 0 else y, core)],
            z_peers[k],
            2 + core,
        )
    def ring(far, owner):
        strips = every.at[part(1 - zh if far else zh, along, owner)]
        first = 30 + (far * 2 + owner) * 3
        for k in range(3):
            start(first + k, strips, strips, gather_peer(k + 1), first + k)

    ring(0, core)
    start(0, table_out, table.at[along, core], sibling, 0)
    start(4, wm.at[0], wm.at[1], ch_same, 4)
    start(5, wl_part.at[0], wl_part.at[1], ch_same, 5)
    start(6, ws_part.at[0], ws_part.at[1], ch_same, 6)
    loading[13].start()
    loading[14].start()
    loading[6].wait()
    loading[7].wait()
    first_layer(0)

    arrived(1, every.at[part(zh, along, 1 - core)])
    ring(0, 1 - core)
    arrived(0, table.at[across, 1 - core])
    for step in range(1, 4):
        start(8 + step, table.at[across], table.at[across], select_peer(step), 8 + step)
    for owner in range(2):
        arrived(2 + owner, every.at[part(1 - zh, along, owner)])
        ring(1, owner)
    first_layer(1)
    before = lax.rem(along + 3, 4)
    after = lax.rem(along + 1, 4)
    opposite = lax.rem(along + 2, 4)
    for step in range(1, 4):
        arrived(8 + step, table.at[lax.rem(across + 4 - step, 4)])
    to_scalars = pltpu.make_async_copy(table, table_s, local_sem.at[len(loads)])
    to_scalars.start()
    first_layer(2)
    arrived(4, wm.at[1])
    arrived(5, wl_part.at[1])
    arrived(6, ws_part.at[1])
    for number in (11, 12):
        loading[number].wait()
    for i in range(3):
        for half in range(2):
            at = i * 128 + half * 64
            for j in range(3):
                source = (i * 3 + j) * 64
                wbt[at : at + 64, j * 128 : j * 128 + 128] = wm[half, source : source + 64, :]
        wf[i] = wbt[i * 128 : i * 128 + 128, :].astype(F32).T.astype(BF)
    own128 = pl.multiple_of(ch * 128, 128)
    other128 = pl.multiple_of((1 - ch) * 128, 128)
    wl[0:64, :] = wl_part[0]
    wl[64:128, :] = wl_part[1]
    ws[pl.ds(own128, 128), :] = ws_part[0]
    ws[pl.ds(other128, 128), :] = ws_part[1]
    bias = mid_bias_n[...]
    swapped = jnp.concatenate([bias[:, 64:128], bias[:, 0:64]], axis=1)
    mid_bias[...] = jnp.where(ch == 0, bias, swapped)
    for ref in (g_first, g_mid, g_last, g_side, g_first_bias, g_mid_bias, g_last_bias):
        ref[...] = jnp.zeros_like(ref)
    blank = jnp.zeros((32, 128), BF)
    for line, lanes in ((32, 0), (33, 0), (0, 128), (33, 128), (0, 256), (1, 256)):
        mid_delta[line, :, lanes : lanes + 128] = blank
    to_scalars.wait()
    for far, plane in enumerate((zh, 1 - zh)):
        for owner in range(2):
            first = 30 + (far * 2 + owner) * 3
            for k, origin in enumerate((before, opposite, after)):
                arrived(first + k, every.at[part(plane, origin, owner)])

    first_dir = 1 + 2 * core
    second_dir = 6 - 2 * core
    rows16 = lax.broadcasted_iota(jnp.int32, (16, 128), 0)

    got = (got_first, got_second)

    def pack_round(step, turn):
        wanted = lax.rem(across + step, 4)
        into = pack.at[step, turn] if step else got[turn].at[0]

        def pack_tile(slot, corners):
            owner, tile = slot // 2, turn + 2 * (slot % 2)

            def held(d):
                return table_s[wanted, owner, tile, d] & 63

            at = slot * 64
            into[pl.ds(at, 32), :] = every[held(first_dir), 1]
            into[pl.ds(at + 32, 32), :] = every[held(second_dir), 0]
            for k, (d, which, line) in enumerate(CORNERS):
                rows = every[held(d), which, 16 * (line // 16) : 16 * (line // 16) + 16, :]
                row = rows.astype(F32)[line % 16 : line % 16 + 1]
                corners = jnp.where(rows16 == slot * 4 + k, row, corners)
            return corners

        corners = jnp.zeros((16, 128), F32)
        for slot in range(4):
            corners = pack_tile(slot, corners)
        into[256:272, :] = corners.astype(BF)
        if step:
            number = 17 + turn * 3 + step
            start(number, pack.at[step, turn], got[turn].at[step], select_peer(step), number)

    def finish_round(owner, turn):
        def finish_tile(k, corners):
            slot, tile = owner * 2 + k, turn + 2 * k

            def chosen(d, rows):
                from_step = (across + 4 - (table_s[across, owner, tile, d] >> 6)) & 3
                return got[turn][from_step, rows, :]

            at = pl.multiple_of(slot * 64, 64)
            to = k * 64
            piece[turn, owner, pl.ds(to, 32), :] = chosen(first_dir, pl.ds(at, 32))
            piece[turn, owner, pl.ds(to + 32, 32), :] = chosen(second_dir, pl.ds(at + 32, 32))
            for c, (d, _, _) in enumerate(CORNERS):
                rows = chosen(d, slice(256, 272)).astype(F32)
                corners = jnp.where(rows16 == slot * 4 + c, rows, corners)
            return corners

        corners = jnp.zeros((16, 128), F32)
        for k in range(2):
            corners = finish_tile(k, corners)
        half = jnp.where(owner == 0, corners[0:8], corners[8:16])
        both = jnp.concatenate([half, half], axis=0)
        piece[turn, owner, 128:144, :] = both.astype(BF)

    for turn in range(2):
        for step in (2, 1, 3):
            pack_round(step, turn)
    pack_round(0, 0)
    pack_round(0, 1)
    first_layer(3)
    for turn in range(2):
        for step in range(1, 4):
            arrived(17 + turn * 3 + step, got[turn].at[step])
        for owner, copies in (
            (1 - core, ((0, ch_cross), (1, sibling))),
            (core, ((2, ch_same),)),
        ):
            finish_round(owner, turn)
            for k, peer in copies:
                number = 24 + turn * 3 + k
                start(number, piece.at[turn, owner], halo.at[core, ch, turn], peer, number)
        halo[core, ch, turn] = piece[turn, core]

    def halo_arrived(turn):
        arrived(24 + turn * 3, halo.at[1 - core, 1 - ch, turn])
        arrived(25 + turn * 3, halo.at[1 - core, ch, turn])
        arrived(26 + turn * 3, halo.at[core, 1 - ch, turn])

    loading[1].wait()


    def here(tile, direction):
        return jnp.where(near_s[tile, direction] < 256, 1.0, 0.0).astype(F32)

    def rim_features(turn, which):
        rows = pl.ds(pl.multiple_of(which * 64, 64), 64)
        parts = [(0, rows), (1, rows), (0, slice(128, 144))]
        return jnp.concatenate(
            [jnp.concatenate([halo[r, h, turn, at, :] for h in range(2)], axis=1) for r, at in parts],
            axis=0,
        )

    def pad(tile, turn, which):
        pre = dot(rim_features(turn, which), w1[...]) + b1[...]
        sig = sigmoid(pre)
        act = pre * sig
        rim_slope[...] = sig + act * (1.0 - sig)
        rim[...] = act
        padded[tile, 0, 8:40, :] = act[0:32] * here(tile, 1)
        padded[tile, 33, 8:40, :] = act[32:64] * here(tile, 6)
        padded[tile, 1:33, 7:8, :] = (act[64:96] * here(tile, 3)).reshape(32, 1, 128)
        padded[tile, 1:33, 40:41, :] = (act[96:128] * here(tile, 4)).reshape(32, 1, 128)
        for k, (d, line, column) in enumerate(PLACES):
            row = rim[pl.ds(128 + which * 4 + k, 1), :]
            padded[tile, line, column : column + 1, :] = row * here(tile, d)
        for j in range(3):
            patches[:, :, j * 128 : j * 128 + 128] = padded[tile, :, 7 + j : 39 + j, :].astype(BF)

    high = CHUNK // 32

    def forward(tile, number):
        row = pl.multiple_of(number * CHUNK, CHUNK)
        line = number * high
        views = [patches[pl.ds(line + i, high)].reshape(CHUNK, 384) for i in range(3)]
        mid_pre = mid_bias[...] + dot(views[0], wf[0]) + dot(views[1], wf[1]) + dot(views[2], wf[2])
        mid_sig = sigmoid(mid_pre)
        mid_val = mid_pre * mid_sig
        mid_act = mid_val.astype(BF)
        x_part = feat[tile, pl.ds(line, high)].reshape(CHUNK, 256)
        out_pre = dot(mid_act, wl[...]) + dot(x_part, ws[...]) + last_bias[...]
        sig = sigmoid(out_pre)
        val = out_pre * sig
        out[tile, pl.ds(row, CHUNK), :] = val.astype(BF)
        return row, line, views, mid_sig, mid_val, mid_act, x_part, sig, val

    def forward_tile(tile, first, last):
        def body(number, carry):
            forward(tile, number)
            return carry

        lax.fori_loop(first, last, body, 0, unroll=True)

    def whole_tile(k, carry):
        tile = 2 * ch + k
        halo_arrived(k)
        pad(tile, k, ch)

        def body(number, inner):
            row, line, views, mid_sig, mid_val, mid_act, x_part, sig, val = forward(tile, number)
            slope = sig + val * (1.0 - sig)
            grad_out = (cot[k, pl.ds(row, CHUNK), :].astype(F32) * scale * slope).astype(BF)
            g_last[...] += dot_tn(mid_act, grad_out)
            g_side[...] += dot(feat_t[k, :, pl.ds(row, CHUNK)], grad_out)
            g_last_bias[...] += grad_out.astype(F32).reshape(CHUNK // 8, 8, 512).sum(axis=0)
            mid_back = dot_nt(grad_out, wl[...])
            delta = (mid_back * (mid_sig + mid_val * (1.0 - mid_sig))).astype(BF)
            g_mid_bias[...] += delta.astype(F32).reshape(CHUNK // 8, 8, 128).sum(axis=0)
            for i in range(3):
                g_mid[i] += dot_tn(delta, views[i])
            for i in range(3):
                mid_delta[pl.ds(line + i, high), :, i * 128 : i * 128 + 128] = delta.reshape(
                    high, 32, 128
                )
            return inner

        lax.fori_loop(0, 1024 // CHUNK, body, 0, unroll=True)

        back = dot(mid_delta[...].reshape(1088, 384), wbt[...]).reshape(34, 32, 384)
        spread[:, 0:8, :] = jnp.zeros((34, 8, 128), F32)
        spread[:, 40:48, :] = jnp.zeros((34, 8, 128), F32)
        spread[:, 8:40, :] = back[:, :, 128:256]
        spread[:, 7:39, :] += back[:, :, 0:128]
        spread[:, 9:41, :] += back[:, :, 256:384]

        delta = (spread[1:33, 8:40, :].reshape(1024, 128) * first_slope[k]).astype(BF)
        rim[...] = jnp.zeros_like(rim)
        rim[0:32, :] = spread[0, 8:40, :] * here(tile, 1)
        rim[32:64, :] = spread[33, 8:40, :] * here(tile, 6)
        rim[64:96, :] = spread[1:33, 7:8, :].reshape(32, 128) * here(tile, 3)
        rim[96:128, :] = spread[1:33, 40:41, :].reshape(32, 128) * here(tile, 4)
        for c, (d, line, column) in enumerate(PLACES):
            row = spread[line, column : column + 1, :]
            rim[pl.ds(128 + ch * 4 + c, 1), :] = row * here(tile, d)
        delta_rim = (rim[...] * rim_slope[...]).astype(BF)
        g_first[...] += dot(feat_t[k], delta) + dot_tn(rim_features(k, ch), delta_rim)
        g_first_bias[...] += delta.astype(F32).reshape(128, 8, 128).sum(axis=0)
        g_first_bias[...] += delta_rim.astype(F32).reshape(18, 8, 128).sum(axis=0)
        return carry

    loading[13].wait()
    loading[14].wait()
    lax.fori_loop(0, 2, whole_tile, 0)


    g_first_t[...] = g_first[...].T
    bias_first = jnp.sum(g_first_bias[...], axis=0, keepdims=True)
    bias_mid = jnp.sum(g_mid_bias[...], axis=0, keepdims=True)
    bias_last = jnp.sum(g_last_bias[...], axis=0, keepdims=True)
    for half in range(2):
        whose = ch if half == 0 else 1 - ch
        start64 = pl.multiple_of(whose * 64, 64)
        start128 = pl.multiple_of(whose * 128, 128)
        order = slice(half * 64, half * 64 + 64)
        for k in range(2):
            at = ROW_FIRST + k * 64
            lanes = slice(k * 128, k * 128 + 128)
            grads[half, at : at + 64, :] = g_first_t[pl.ds(start64, 64), lanes].astype(BF)
        for i in range(3):
            for j in range(3):
                at = ROW_MID + (i * 3 + j) * 64
                lanes = slice(j * 128, j * 128 + 128)
                grads[half, at : at + 64, :] = g_mid[i, order, lanes].astype(BF)
        for k in range(4):
            lanes = slice(k * 128, k * 128 + 128)
            at = ROW_LAST + k * 64
            grads[half, at : at + 64, :] = g_last[order, lanes].astype(BF)
            at = ROW_SIDE + k * 128
            grads[half, at : at + 128, :] = g_side[pl.ds(start128, 128), lanes].astype(BF)
        mid_row = bias_mid
        if half == 1:
            mid_row = jnp.concatenate([bias_mid[:, 64:128], bias_mid[:, 0:64]], axis=1)
        rows = jnp.where(rows16 == 0, bias_first, jnp.where(rows16 == 1, mid_row, 0.0))
        for k in range(4):
            rows = jnp.where(rows16 == 2 + k, bias_last[:, k * 128 : k * 128 + 128], rows)
        grads[half, ROW_BIAS : ROW_BIAS + 16, :] = rows.astype(BF)
        grads[half, ROW_BIAS + 16 : ROWS, :] = jnp.zeros((ROWS - ROW_BIAS - 16, 128), BF)


    def hand(number, source, target, peer):
        made = pltpu.make_async_remote_copy(
            src_ref=source,
            dst_ref=target,
            send_sem=sum_send_sem.at[number],
            recv_sem=sum_recv_sem.at[number],
            device_id=peer,
            device_id_type=MESH,
        )
        made.start()
        sent.append(made)
        return made

    third = lax.rem(2 + 2 * ch, 4)
    fourth = lax.rem(3 + 2 * ch, 4)
    count = 1024 // CHUNK

    own_rows = pl.multiple_of(core * CORE_ROWS, CORE_ROWS)
    other_rows = pl.multiple_of((1 - core) * CORE_ROWS, CORE_ROWS)
    swap = hand(0, grads.at[:, pl.ds(other_rows, CORE_ROWS)], from_core, sibling)
    pad(third, 0, 1 - ch)
    swap.wait_recv()
    for half in range(2):
        added = grads[half, pl.ds(own_rows, CORE_ROWS), :].astype(F32) + from_core[half].astype(F32)
        by_piece[:, half] = added.astype(BF).reshape(16, PIECE, 128)
    plane = []
    for step in FAR_FIRST:
        piece_of = by_piece.at[plane_place(step)]
        plane.append((step, hand(step, piece_of, from_plane.at[step], plane_peer(step))))
    forward_tile(third, 0, count)
    added = by_piece[own_place].astype(F32)
    for step, made in reversed(plane):
        made.wait_recv()
        added = added + from_plane[step].astype(F32)
    mine[...] = added.astype(BF)
    hops = []
    for k, (half, peer) in enumerate(((0, z_even), (1, ch_same), (1, z_odd))):
        hops.append(hand(16 + k, mine.at[half], from_z.at[k], peer))
    pad(fourth, 1, 1 - ch)
    forward_tile(fourth, 0, count // 2)
    added = added[0]
    for k, made in enumerate(hops):
        made.wait_recv()
        added = added + from_z[k].astype(F32)
    at = pl.multiple_of(own_rows + own_place * PIECE, 16)
    total[pl.ds(at, PIECE), :] = added.astype(BF)
    def cross(step):
        origin = plane_place(step, back=True)
        rows = total.at[pl.ds(pl.multiple_of(own_rows + origin * PIECE, 16), PIECE)]
        return hand(34 + step, rows, rows, sibling)

    backs, crossings = [], []
    for step in FAR_FIRST:
        here_too = total.at[pl.ds(at, PIECE)]
        backs.append((step, hand(18 + step, here_too, here_too, plane_peer(step))))
    crossings.append(cross(0))
    forward_tile(fourth, count // 2, count)
    for step, made in reversed(backs):
        made.wait_recv()
        crossings.append(cross(step))
    for made in crossings:
        made.wait_recv()
    for made in sent:
        made.wait_send()


def block(*operands):
    scale = 1.0 / math.sqrt(4096)
    anywhere = pl.BlockSpec(memory_space=pl.ANY)

    def kernel(*refs):
        block_kernel(scale, *refs)

    return pl.pallas_call(
        kernel,
        in_specs=[anywhere] * 10,
        out_specs=(pl.BlockSpec(memory_space=pltpu.VMEM),) * 2,
        out_shape=(
            jax.ShapeDtypeStruct((4, 1024, 512), BF),
            jax.ShapeDtypeStruct((ROWS, 128), BF),
        ),
        scratch_shapes=[
            pltpu.VMEM((4, 32, 32, 256), BF),
            pltpu.VMEM((2, 1024, 512), BF),
            pltpu.VMEM((4, 8), jnp.int32),
            pltpu.SMEM((4, 8), jnp.int32),
            pltpu.VMEM((256, 128), BF),
            pltpu.VMEM((1, 128), F32),
            pltpu.VMEM((2, 576, 128), BF),
            pltpu.VMEM((1, 128), F32),
            pltpu.VMEM((2, 64, 512), BF),
            pltpu.VMEM((2, 128, 512), BF),
            pltpu.VMEM((1, 512), F32),
            pltpu.VMEM((512, 128), F32),
            pltpu.VMEM((2, 2, 4, 2, 32, 128), BF),
            pltpu.VMEM((4, 2, 8, 128), jnp.int32),
            pltpu.VMEM((8, 128), jnp.int32),
            pltpu.SMEM((4, 2, 8, 128), jnp.int32),
            pltpu.VMEM((64, 2, 32, 128), BF),
            pltpu.VMEM((4, 2, 272, 128), BF),
            pltpu.VMEM((4, 272, 128), BF),
            pltpu.VMEM((4, 272, 128), BF),
            pltpu.VMEM((2, 2, 144, 128), BF),
            pltpu.VMEM((2, 2, 2, 144, 128), BF),
            pltpu.VMEM((1, 128), F32),
            pltpu.VMEM((3, 384, 128), BF),
            pltpu.VMEM((384, 384), BF),
            pltpu.VMEM((128, 512), BF),
            pltpu.VMEM((256, 512), BF),
            pltpu.VMEM((2, 1024, 128), F32),
            pltpu.VMEM((2, 256, 1024), BF),
            pltpu.VMEM((144, 128), F32),
            pltpu.VMEM((4, 34, 48, 128), F32),
            pltpu.VMEM((34, 32, 384), BF),
            pltpu.VMEM((34, 32, 384), BF),
            pltpu.VMEM((34, 48, 128), F32),
            pltpu.VMEM((144, 128), F32),
            pltpu.VMEM((256, 128), F32),
            pltpu.VMEM((3, 128, 384), F32),
            pltpu.VMEM((128, 512), F32),
            pltpu.VMEM((256, 512), F32),
            pltpu.VMEM((8, 128), F32),
            pltpu.VMEM((8, 128), F32),
            pltpu.VMEM((8, 512), F32),
            pltpu.VMEM((128, 256), F32),
            pltpu.VMEM((2, ROWS, 128), BF),
            pltpu.VMEM((2, CORE_ROWS, 128), BF),
            pltpu.VMEM((16, 2, PIECE, 128), BF),
            pltpu.VMEM((16, 2, PIECE, 128), BF),
            pltpu.VMEM((2, PIECE, 128), BF),
            pltpu.VMEM((3, PIECE, 128), BF),
            pltpu.SemaphoreType.DMA((16,)),
            pltpu.SemaphoreType.DMA((42,)),
            pltpu.SemaphoreType.DMA((42,)),
            pltpu.SemaphoreType.DMA((50,)),
            pltpu.SemaphoreType.DMA((50,)),
        ],
        compiler_params=pltpu.CompilerParams(
            collective_id=0, has_side_effects=True, vmem_limit_bytes=44 * 2**20
        ),
    )(*[pltpu.with_memory_space_constraint(a, pltpu.HBM) for a in operands])


def finish_kernel(
    out,
    total,
    output,
    g_first,
    g_first_bias,
    g_mid,
    g_mid_bias,
    g_last,
    g_side,
    g_last_bias,
    first_v,
    mid_v,
    last_v,
    side_v,
    out_sem,
):
    writes = [pltpu.make_async_copy(out.at[k], output.at[k], out_sem.at[k]) for k in range(PARTS)]
    for made in writes:
        made.start()

    def send(number, source, target):
        made = pltpu.make_async_copy(source, target, out_sem.at[PARTS + number])
        made.start()
        writes.append(made)

    def rows(at, count):
        return total[at : at + count, :].astype(F32)

    for k in range(4):
        lanes = slice(k * 128, k * 128 + 128)
        side_v[:, lanes] = rows(ROW_SIDE + k * 128, 128)
        last_v[:, lanes] = rows(ROW_LAST + k * 64, 64)
    send(0, side_v, g_side)
    send(1, last_v, g_last)
    for k in range(9):
        mid_v[k // 3, k % 3] = rows(ROW_MID + k * 64, 64)
    send(2, mid_v, g_mid)
    for k in range(2):
        first_v[:, k * 128 : k * 128 + 128] = rows(ROW_FIRST + k * 64, 64)
    send(3, first_v, g_first)
    bias = rows(ROW_BIAS, 16)
    for k in range(4):
        lanes = slice(k * 128, k * 128 + 128)
        g_last_bias[:, lanes] = bias[2 + k : 3 + k, :]
    ch = lax.axis_index("ch")
    g_first_bias[...] = jnp.where(ch == 0, bias[0:1, 0:64], bias[0:1, 64:128])
    g_mid_bias[...] = bias[1:2, 0:64]
    for made in writes:
        made.wait()


def finish(out, total):
    vmem = pl.BlockSpec(memory_space=pltpu.VMEM)
    anywhere = pl.BlockSpec(memory_space=pl.ANY)
    return pl.pallas_call(
        finish_kernel,
        in_specs=[vmem, vmem],
        out_specs=(anywhere, anywhere, vmem, anywhere, vmem, anywhere, anywhere, vmem),
        out_shape=(
            jax.ShapeDtypeStruct(out.shape, BF),
            *[
                jax.ShapeDtypeStruct(shape, F32)
                for shape in (
                    (64, 256),
                    (1, 64),
                    (3, 3, 64, 128),
                    (1, 64),
                    (64, 512),
                    (128, 512),
                    (1, 512),
                )
            ],
        ),
        scratch_shapes=[
            pltpu.VMEM((64, 256), F32),
            pltpu.VMEM((3, 3, 64, 128), F32),
            pltpu.VMEM((64, 512), F32),
            pltpu.VMEM((128, 512), F32),
            pltpu.SemaphoreType.DMA((PARTS + 4,)),
        ],
        compiler_params=pltpu.CompilerParams(vmem_limit_bytes=16 * 2**20),
    )(out, total)


def per_device(
    features,
    cotangent,
    neighbours,
    first_weight,
    first_bias,
    mid_weight,
    mid_bias,
    last_weight,
    side_weight,
    last_bias,
):
    out, total = block(
        features,
        cotangent.reshape(4096, 512),
        neighbours,
        first_weight,
        first_bias.reshape(1, 128),
        mid_weight.transpose(0, 1, 3, 2).reshape(576, 128),
        mid_bias.reshape(1, 128),
        last_weight,
        side_weight,
        last_bias.reshape(1, 512),
    )
    output, g_first, g_first_bias, g_mid, g_mid_bias, g_last, g_side, g_last_bias = finish(
        out.reshape(PARTS, 4096 // PARTS, 512), total
    )
    return (
        output.reshape(4, 32, 32, 512),
        g_first.T,
        g_first_bias.reshape(64),
        g_mid.transpose(0, 1, 3, 2),
        g_mid_bias.reshape(64),
        g_last,
        g_side,
        g_last_bias.reshape(512),
    )


def solution(mesh):
    return jax.shard_map(
        per_device,
        mesh=mesh,
        in_specs=(
            P("tile", None, None, None),
            P("tile", None, None, None),
            P("tile", None),
            P(),
            P(),
            P(None, None, None, "ch"),
            P(),
            P("ch", None),
            P("ch", None),
            P(),
        ),
        out_specs=(
            P("tile", None, None, None),
            P(None, "ch"),
            P("ch"),
            P(None, None, None, "ch"),
            P("ch"),
            P("ch", None),
            P("ch", None),
            P(),
        ),
        check_vma=False,
    )
```
